32 devices in a mesh: branch: 4 (over y, x), rows: 8 (over z, core).
Axes of the slice: x: 2, y: 2, z: 4, core: 2. Of those that a mesh axis runs over, the one named last changes fastest.
Arguments:
- maps_four: bfloat16 [48, 64, 1024], P(None, 'rows', 'branch'), may hold values from -6 to 6
- maps_eight: bfloat16 [96, 32, 512], P(None, 'rows', 'branch'), may hold values from -6 to 6
- maps_sixteen: bfloat16 [192, 16, 256], P(None, 'rows', 'branch'), may hold values from -6 to 6
- maps_thirtytwo: bfloat16 [384, 8, 128], P(None, 'rows', 'branch'), may hold values from -6 to 6
- kernel_four: bfloat16 [3, 3, 48, 48], replicated, may hold values from -0.3125 to 0.3125
- kernel_eight: bfloat16 [3, 3, 96, 96], replicated, may hold values from -0.21875 to 0.21875
- kernel_sixteen: bfloat16 [3, 3, 192, 192], replicated, may hold values from -0.15625 to 0.15625
- kernel_thirtytwo: bfloat16 [3, 3, 384, 384], replicated, may hold values from -0.109375 to 0.109375
- gain_four: float32 [48], replicated, may hold values from 0.1 to 1.9
- gain_eight: float32 [96], replicated, may hold values from 0.1 to 1.9
- gain_sixteen: float32 [192], replicated, may hold values from 0.1 to 1.9
- gain_thirtytwo: float32 [384], replicated, may hold values from 0.1 to 1.9
- mixer_four: bfloat16 [48, 672], replicated, may hold values from -0.25 to 0.25
- mixer_eight: bfloat16 [96, 624], replicated, may hold values from -0.25 to 0.25
- mixer_sixteen: bfloat16 [192, 528], replicated, may hold values from -0.25 to 0.25
- mixer_thirtytwo: bfloat16 [384, 336], replicated, may hold values from -0.3125 to 0.3125
- cotan_four: bfloat16 [48, 64, 1024], P(None, 'rows', 'branch'), may hold values from -6 to 6
- cotan_eight: bfloat16 [96, 32, 512], P(None, 'rows', 'branch'), may hold values from -6 to 6
- cotan_sixteen: bfloat16 [192, 16, 256], P(None, 'rows', 'branch'), may hold values from -6 to 6
- cotan_thirtytwo: bfloat16 [384, 8, 128], P(None, 'rows', 'branch'), may hold values from -6 to 6
Outputs:
- merged_four: bfloat16 [48, 64, 1024], P(None, 'rows', 'branch')
- merged_eight: bfloat16 [96, 32, 512], P(None, 'rows', 'branch')
- merged_sixteen: bfloat16 [192, 16, 256], P(None, 'rows', 'branch')
- merged_thirtytwo: bfloat16 [384, 8, 128], P(None, 'rows', 'branch')
- backprop_four: bfloat16 [48, 64, 1024], P(None, 'rows', 'branch')
- backprop_eight: bfloat16 [96, 32, 512], P(None, 'rows', 'branch')
- backprop_sixteen: bfloat16 [192, 16, 256], P(None, 'rows', 'branch')
- backprop_thirtytwo: bfloat16 [384, 8, 128], P(None, 'rows', 'branch')
- kernelgrad_four: bfloat16 [3, 3, 48, 48], replicated
- kernelgrad_eight: bfloat16 [3, 3, 96, 96], replicated
- kernelgrad_sixteen: bfloat16 [3, 3, 192, 192], replicated
- kernelgrad_thirtytwo: bfloat16 [3, 3, 384, 384], replicated
The draws below stay inside these ranges and needn't reach their ends.
All inputs are finite; a program needn't handle non-finite values.
Results may differ from the reference program's by a relative error of at most 0.015.
Values may be sent and summed in bfloat16 or wider, within the bound.
No kernel may reach another device: no remote copies, remote signals or barrier semaphores. Data moves between devices by JAX's collectives and lax.ppermute only.
A program may use at most 128 MiB of HBM per device.

```python
import math
import jax
import jax.numpy as jnp
from jax import lax

CH4 = 48
CH8 = 96
CH16 = 192
CH32 = 384
H4 = 64
W4 = 1024
H8 = 32
W8 = 512
H16 = 16
W16 = 256
H32 = 8
W32 = 128
MERGE4 = 672
MERGE8 = 624
MERGE16 = 528
MERGE32 = 336


def level_of(own_key, extent, shards, low, top_value):
    def one(dim, blocks):
        steps = jax.random.uniform(jax.random.fold_in(jax.random.fold_in(own_key, 6), dim), (blocks,), jnp.float32, low / len(shards), top_value / len(shards))
        return jnp.repeat(jnp.exp(steps), extent[dim] // blocks).reshape((-1,) + (1,) * (len(extent) - dim - 1))

    gain = one(*shards[0])
    for cut in shards[1:]:
        gain = gain * one(*cut)
    return gain


def normal_values(rng, extent, width, reach, split=(), held_as=jnp.bfloat16):
    values = jax.random.normal(rng, extent, jnp.float32) * width
    if len(split) > 0:
        values = level_of(rng, extent, split, -0.22, 0.18) * values
    return jnp.clip(values, min=-reach, max=reach).astype(held_as)


def setup_inputs(seed: int = 0) -> dict:
    streams_of = jax.random.split(jax.random.key(seed), 21)
    maps_four = normal_values(streams_of[0], (CH4, H4, W4), 1.0, 6.0, ((1, 8), (2, 4)))
    maps_eight = normal_values(streams_of[1], (CH8, H8, W8), 1.0, 6.0, ((1, 8), (2, 4)))
    maps_sixteen = normal_values(streams_of[2], (CH16, H16, W16), 1.0, 6.0, ((1, 8), (2, 4)))
    maps_thirtytwo = normal_values(streams_of[3], (CH32, H32, W32), 1.0, 6.0, ((1, 8), (2, 4)))
    kernel_four = normal_values(streams_of[4], (3, 3, CH4, CH4), (9 * CH4) ** -0.5, 0.3125)
    kernel_eight = normal_values(streams_of[5], (3, 3, CH8, CH8), (9 * CH8) ** -0.5, 0.21875)
    kernel_sixteen = normal_values(streams_of[6], (3, 3, CH16, CH16), (9 * CH16) ** -0.5, 0.15625)
    kernel_thirtytwo = normal_values(streams_of[7], (3, 3, CH32, CH32), (9 * CH32) ** -0.5, 0.109375)
    gain_four = jnp.clip(1.0 + 0.18 * jax.random.normal(streams_of[8], (CH4,), jnp.float32), 0.1, 1.9)
    gain_eight = jnp.clip(1.0 + 0.18 * jax.random.normal(streams_of[9], (CH8,), jnp.float32), 0.1, 1.9)
    gain_sixteen = jnp.clip(1.0 + 0.18 * jax.random.normal(streams_of[10], (CH16,), jnp.float32), 0.1, 1.9)
    gain_thirtytwo = jnp.clip(1.0 + 0.18 * jax.random.normal(streams_of[11], (CH32,), jnp.float32), 0.1, 1.9)
    mixer_four = normal_values(streams_of[12], (CH4, MERGE4), MERGE4 ** -0.5, 0.25)
    mixer_eight = normal_values(streams_of[13], (CH8, MERGE8), MERGE8 ** -0.5, 0.25)
    mixer_sixteen = normal_values(streams_of[14], (CH16, MERGE16), MERGE16 ** -0.5, 0.25)
    mixer_thirtytwo = normal_values(streams_of[15], (CH32, MERGE32), MERGE32 ** -0.5, 0.3125)
    cotan_four = normal_values(streams_of[16], (CH4, H4, W4), 1.0, 6.0, ((1, 8), (2, 4)))
    cotan_eight = normal_values(streams_of[17], (CH8, H8, W8), 1.0, 6.0, ((1, 8), (2, 4)))
    cotan_sixteen = normal_values(streams_of[18], (CH16, H16, W16), 1.0, 6.0, ((1, 8), (2, 4)))
    cotan_thirtytwo = normal_values(streams_of[19], (CH32, H32, W32), 1.0, 6.0, ((1, 8), (2, 4)))
    return {"maps_four": maps_four, "maps_eight": maps_eight, "maps_sixteen": maps_sixteen, "maps_thirtytwo": maps_thirtytwo, "kernel_four": kernel_four, "kernel_eight": kernel_eight, "kernel_sixteen": kernel_sixteen, "kernel_thirtytwo": kernel_thirtytwo, "gain_four": gain_four, "gain_eight": gain_eight, "gain_sixteen": gain_sixteen, "gain_thirtytwo": gain_thirtytwo, "mixer_four": mixer_four, "mixer_eight": mixer_eight, "mixer_sixteen": mixer_sixteen, "mixer_thirtytwo": mixer_thirtytwo, "cotan_four": cotan_four, "cotan_eight": cotan_eight, "cotan_sixteen": cotan_sixteen, "cotan_thirtytwo": cotan_thirtytwo}


def forward_taps(padded, kernel):
    channels = padded.shape[0]
    height = padded.shape[1] - 2
    columns = padded.shape[2] - 2
    summed = jnp.zeros((kernel.shape[2], height * columns), jnp.float32)
    for row_off in range(3):
        for col_off in range(3):
            window = padded[:, row_off:row_off + height, col_off:col_off + columns].reshape(channels, height * columns)
            summed = summed + jnp.dot(kernel[row_off, col_off], window, preferred_element_type=jnp.float32)
    return summed.reshape(kernel.shape[2], height, columns)

def adjoint_taps(padded, kernel):
    channels = padded.shape[0]
    height = padded.shape[1] - 2
    columns = padded.shape[2] - 2
    summed = jnp.zeros((kernel.shape[3], height * columns), jnp.float32)
    for row_off in range(3):
        for col_off in range(3):
            window = padded[:, 2 - row_off:2 - row_off + height, 2 - col_off:2 - col_off + columns].reshape(channels, height * columns)
            summed = summed + lax.dot_general(kernel[row_off, col_off], window, (((0,), (0,)), ((), ())), preferred_element_type=jnp.float32)
    return summed.reshape(kernel.shape[3], height, columns)

def kernel_taps(padded, gradient):
    channels = padded.shape[0]
    outputs = gradient.shape[0]
    height = gradient.shape[1]
    columns = gradient.shape[2]
    flattened = gradient.reshape(outputs, height * columns)
    tap_list = []
    for row_off in range(3):
        for col_off in range(3):
            window = padded[:, row_off:row_off + height, col_off:col_off + columns].reshape(channels, height * columns)
            tap_list.append(lax.dot_general(flattened, window, (((1,), (1,)), ((), ())), preferred_element_type=jnp.float32))
    return jnp.stack(tap_list).reshape(3, 3, outputs, channels)

def upsample(values, factor):
    channels, height, columns = values.shape
    spread_out = jnp.broadcast_to(values[:, :, None, :, None], (channels, height, factor, columns, factor))
    return spread_out.reshape(channels, height * factor, columns * factor)

def source_offset(channel_counts, target, source):
    return sum((channel_counts[index] for index in range(source) if index != target))

def merged_maps(results, mixers, target):
    channel_counts = [item.shape[0] for item in results]
    summed = results[target].astype(jnp.float32)
    height = results[target].shape[1]
    columns = results[target].shape[2]
    for source in range(4):
        if source == target:
            continue
        width_in = channel_counts[source]
        offset = source_offset(channel_counts, target, source)
        mixer_block = mixers[target][:, offset:offset + width_in]
        if source > target:
            factor = 2 ** (source - target)
            projected = jnp.dot(mixer_block, results[source].reshape(width_in, -1), preferred_element_type=jnp.float32)
            projected = projected.reshape(-1, results[source].shape[1], results[source].shape[2])
            summed = summed + upsample(projected, factor)
        else:
            factor = 2 ** (target - source)
            pooled = results[source].astype(jnp.float32).reshape(width_in, height, factor, columns, factor).mean(axis=(2, 4)).astype(jnp.bfloat16)
            projected = jnp.dot(mixer_block, pooled.reshape(width_in, -1), preferred_element_type=jnp.float32)
            summed = summed + projected.reshape(-1, height, columns)
    return summed

def merged_adjoint(cotans, mixers, source):
    channel_counts = [item.shape[0] for item in cotans]
    summed = cotans[source].astype(jnp.float32)
    width_in = channel_counts[source]
    height = cotans[source].shape[1]
    columns = cotans[source].shape[2]
    for target in range(4):
        if target == source:
            continue
        offset = source_offset(channel_counts, target, source)
        mixer_block = mixers[target][:, offset:offset + width_in]
        outward = channel_counts[target]
        if source > target:
            factor = 2 ** (source - target)
            blocksum = cotans[target].astype(jnp.float32).reshape(outward, height, factor, columns, factor).sum(axis=(2, 4)).astype(jnp.bfloat16)
            projected = lax.dot_general(mixer_block, blocksum.reshape(outward, -1), (((0,), (0,)), ((), ())), preferred_element_type=jnp.float32)
            summed = summed + projected.reshape(width_in, height, columns)
        else:
            factor = 2 ** (target - source)
            projected = lax.dot_general(mixer_block, cotans[target].reshape(outward, -1), (((0,), (0,)), ((), ())), preferred_element_type=jnp.float32)
            projected = projected.reshape(width_in, cotans[target].shape[1], cotans[target].shape[2])
            summed = summed + upsample(projected, factor) / float(factor * factor)
    return summed

def reference(maps_four, maps_eight, maps_sixteen, maps_thirtytwo, kernel_four, kernel_eight, kernel_sixteen, kernel_thirtytwo, gain_four, gain_eight, gain_sixteen, gain_thirtytwo, mixer_four, mixer_eight, mixer_sixteen, mixer_thirtytwo, cotan_four, cotan_eight, cotan_sixteen, cotan_thirtytwo):
    features = [maps_four, maps_eight, maps_sixteen, maps_thirtytwo]
    kernels = [kernel_four, kernel_eight, kernel_sixteen, kernel_thirtytwo]
    gain_list = [gain_four, gain_eight, gain_sixteen, gain_thirtytwo]
    mixers = [mixer_four, mixer_eight, mixer_sixteen, mixer_thirtytwo]
    cotans = [cotan_four, cotan_eight, cotan_sixteen, cotan_thirtytwo]
    extended = []
    results = []
    for branch in range(4):
        active = jnp.maximum(features[branch], jnp.zeros((), features[branch].dtype))
        padded = jnp.pad(active, ((0, 0), (1, 1), (1, 1)))
        extended.append(padded)
        response = forward_taps(padded, kernels[branch])
        results.append((features[branch].astype(jnp.float32) + gain_list[branch][:, None, None] * response).astype(jnp.bfloat16))
    merged = [merged_maps(results, mixers, target).astype(jnp.bfloat16) for target in range(4)]
    backward_list = []
    kernel_list = []
    for branch in range(4):
        upstream = merged_adjoint(cotans, mixers, branch)
        scaled = (gain_list[branch][:, None, None] * upstream).astype(jnp.bfloat16)
        padded_grads = jnp.pad(scaled, ((0, 0), (1, 1), (1, 1)))
        adjoint = adjoint_taps(padded_grads, kernels[branch])
        backward = upstream + jnp.where(features[branch] > 0, adjoint, jnp.zeros((), jnp.float32))
        backward_list.append(backward.astype(jnp.bfloat16))
        pixels = features[branch].shape[1] * features[branch].shape[2]
        summed = kernel_taps(extended[branch], scaled)
        kernel_list.append((summed * (1.0 / math.sqrt(pixels))).astype(jnp.bfloat16))
    return (merged[0], merged[1], merged[2], merged[3], backward_list[0], backward_list[1], backward_list[2], backward_list[3], kernel_list[0], kernel_list[1], kernel_list[2], kernel_list[3])
```

```python
import functools
import math

import jax
import jax.numpy as jnp
from jax import lax
from jax.experimental import pallas as pl
from jax.experimental.pallas import tpu as pltpu
from jax.sharding import PartitionSpec as P

BF = jnp.bfloat16
F32 = jnp.float32
LEFT = 8
PACK = 384


def dot(a, b, ca=1, cb=0):
    return lax.dot_general(a, b, (((ca,), (cb,)), ((), ())), preferred_element_type=F32)


def source_offset(channels, target, source):
    return sum(channels[k] for k in range(source) if k != target)


def call(body, outs, args, scratch=(), flops=10**8, nbytes=10**6):
    return pl.pallas_call(
        body,
        out_shape=outs,
        in_specs=[pl.BlockSpec(memory_space=pltpu.VMEM) for _ in args],
        out_specs=[pl.BlockSpec(memory_space=pltpu.VMEM) for _ in outs],
        scratch_shapes=list(scratch),
        compiler_params=pltpu.CompilerParams(vmem_limit_bytes=48 * 1024 * 1024),
        cost_estimate=pl.CostEstimate(flops=flops, bytes_accessed=nbytes, transcendentals=0),
    )(*args)


def sds(shape, dtype):
    return jax.ShapeDtypeStruct(shape, dtype)


def group_matrix(groups, cells, factor, transposed=False):
    shape = (cells, groups) if transposed else (groups, cells)
    g = lax.broadcasted_iota(jnp.int32, shape, 1 if transposed else 0)
    c = lax.broadcasted_iota(jnp.int32, shape, 0 if transposed else 1)
    return jnp.where((c >= g * factor) & (c < g * factor + factor), 1.0, 0.0).astype(BF)


def row_pack(row, channels):
    blocks = PACK // channels
    part = row.shape[0] // blocks
    return jnp.concatenate([row[k * part : (k + 1) * part] for k in range(blocks)], axis=1)


def row_unpack(packed, channels):
    blocks = PACK // channels
    return jnp.concatenate(
        [packed[:, k * channels : (k + 1) * channels] for k in range(blocks)], axis=0
    )


def col_rows(heights):
    starts, at = [], 0
    for h in heights:
        starts.append(at)
        at += h
    return starts


def upstream_kernel(dims, *refs):
    heights, widths, channels = dims
    x_refs, d_refs, g_refs, f_refs = refs[0:4], refs[4:8], refs[8:12], refs[12:16]
    xt4, xt8 = refs[16], refs[17]
    up_refs, sc_refs = refs[18:22], refs[22:26]
    top, bot, left, right = refs[26:30]
    dt = [None] * 4
    xt = [None] * 4
    for b in range(4):
        if b < 2:
            eye = group_matrix(channels[b], channels[b], 1)
            xs = jnp.swapaxes(x_refs[b][...].astype(F32), 0, 1).astype(BF)
            ds = jnp.swapaxes(d_refs[b][...].astype(F32), 0, 1).astype(BF)
            xt[b] = [dot(xs[r], eye, 0, 0).astype(BF) for r in range(heights[b])]
            dt[b] = [dot(ds[r], eye, 0, 0).astype(BF) for r in range(heights[b])]
            for r in range(heights[b]):
                (xt4, xt8)[b][r] = xt[b][r]
        else:
            xt[b] = [x_refs[b][r] for r in range(heights[b])]
            dt[b] = [d_refs[b][r] for r in range(heights[b])]
    mixers = [f_refs[j][...] for j in range(4)]

    def block(j, i):
        off = source_offset(channels, j, i)
        if j == 3:
            return mixers[3][off : off + channels[i]]
        return mixers[j][:, off : off + channels[i]]

    acc = [[dt[i][r].astype(F32) for r in range(heights[i])] for i in range(4)]
    for j in range(4):
        for i in range(j + 1, 4):
            f = 2 ** (i - j)
            pool = group_matrix(widths[i], widths[j], f)
            mat = block(j, i)
            for r in range(heights[i]):
                s = dot(pool, dt[j][r * f])
                for k in range(1, f):
                    s = s + dot(pool, dt[j][r * f + k])
                acc[i][r] = acc[i][r] + dot(s.astype(BF), mat)
        for i in range(j):
            f = 2 ** (j - i)
            spread = group_matrix(widths[j], widths[i], f, True)
            mat = block(j, i)
            for r in range(heights[j]):
                z = dot(spread, dt[j][r]).astype(BF)
                if j == 3:
                    v = dot(z, mat, 1, 1)
                else:
                    v = dot(z, mat)
                v = v * (1.0 / (f * f))
                for k in range(f):
                    acc[i][r * f + k] = acc[i][r * f + k] + v
    starts = col_rows(heights)
    left[...] = jnp.zeros(left.shape, F32).astype(BF)
    right[...] = jnp.zeros(right.shape, F32).astype(BF)
    top[:, 4 * 32 :, :] = jnp.zeros((2, 16, PACK), F32).astype(BF)
    bot[:, 4 * 32 :, :] = jnp.zeros((2, 16, PACK), F32).astype(BF)
    for b in range(4):
        h, w, c = heights[b], widths[b], channels[b]
        gain = g_refs[b][...]
        act, scl = [], []
        for r in range(h):
            up_refs[b][r] = acc[b][r]
            s = (gain * acc[b][r]).astype(BF)
            sc_refs[b][r] = s
            act.append(jnp.maximum(xt[b][r].astype(F32), 0.0))
            scl.append(s.astype(F32))
        for n, rows in enumerate((act, scl)):
            for out, row in ((top, rows[0]), (bot, rows[h - 1])):
                out[n, b * 32 : (b + 1) * 32, :] = row_pack(row, c).astype(BF)
                out[n, 128 + b : 129 + b, :c] = row[0:1].astype(BF)
                out[n, 136 + b : 137 + b, :c] = row[w - 1 : w].astype(BF)
            firsts = jnp.concatenate([row[0:1] for row in rows], axis=0)
            lasts = jnp.concatenate([row[w - 1 : w] for row in rows], axis=0)
            left[n, starts[b] : starts[b] + h, :c] = firsts.astype(BF)
            right[n, starts[b] : starts[b] + h, :c] = lasts.astype(BF)


def fill(scr, n, b, dims, interior, top, bot, left, right):
    heights, widths, channels = dims
    h, w, c = heights[b], widths[b], channels[b]
    start = col_rows(heights)[b]
    for r in range(h):
        scr[r + 1, LEFT : LEFT + w, :] = interior(r)
    for edge, at in ((top, 0), (bot, h + 1)):
        packed = edge[n, b * 32 : (b + 1) * 32, :].astype(F32)
        scr[at, LEFT : LEFT + w, :] = row_unpack(packed, c)
    for edge, at in ((left, LEFT - 1), (right, LEFT + w)):
        vals = edge[n].astype(F32)
        for r in range(h):
            scr[r + 1, at : at + 1, :] = vals[start + r : start + r + 1, :c]
        scr[0, at : at + 1, :] = vals[16 + b : 17 + b, :c]
        scr[h + 1, at : at + 1, :] = vals[24 + b : 25 + b, :c]


def shifted(scr, h, w, q):
    return [scr[r, LEFT - 1 + q : LEFT - 1 + q + w, :].astype(BF) for r in range(h + 2)]


def stack(rows):
    return rows[0] if len(rows) == 1 else jnp.concatenate(rows, axis=0)


def weight_grads_kernel(dims, *refs):
    heights, widths, channels = dims
    x_refs, sc_refs = refs[0:3], refs[3:6]
    top, bot, left, right = refs[6:10]
    out = refs[10]
    scrs = refs[11:14]
    c0, c1, c2 = channels[0], channels[1], channels[2]
    for b in range(3):
        h, w, c = heights[b], widths[b], channels[b]
        fill(
            scrs[b], 0, b, dims,
            lambda r: jnp.maximum(x_refs[b][r].astype(F32), 0.0), top, bot, left, right,
        )
        s_all = stack([sc_refs[b][r] for r in range(h)])
        for q in range(3):
            rows = shifted(scrs[b], h, w, q)
            for p in range(3):
                g = dot(s_all, stack(rows[p : p + h]), 0, 0)
                tap = p * 3 + q
                if b == 2:
                    out[tap * c2 : (tap + 1) * c2, :] = g[:, :128].astype(BF)
                    half = c2 // 2
                    at = 9 * c2 + tap * half
                    both = jnp.concatenate([g[:half, 128:], g[half:, 128:]], axis=1)
                    out[at : at + half, :] = both.astype(BF)
                elif b == 1:
                    at = 9 * c2 * 3 // 2 + tap * c1
                    out[at : at + c1, :c1] = g.astype(BF)
                else:
                    at = 9 * c2 * 3 // 2 + 9 * c1 + (tap // 2) * c0
                    lane = 64 * (tap % 2)
                    out[at : at + c0, lane : lane + c0] = g.astype(BF)


def maps_kernel(dims, *refs):
    heights, widths, channels = dims
    x_refs, sc_refs, up_refs = refs[0:4], refs[4:8], refs[8:12]
    g_refs, f_refs, k_refs = refs[12:16], refs[16:20], refs[20:24]
    top, bot, left, right = refs[24:28]
    merged_refs, back_refs = refs[28:32], refs[32:36]
    act_scrs, grad_scrs = refs[36:40], refs[40:44]
    wide = refs[44:48]
    units = []

    def emit(b, out, rows):
        if b >= 2:
            for r in range(heights[b]):
                out[r] = rows[r].astype(BF)
            return
        stage = wide[b]
        for r in range(heights[b]):
            stage[r] = rows[r].T
        out[...] = jnp.swapaxes(stage[...], 0, 1).astype(BF)

    for b in range(4):
        h, w, c = heights[b], widths[b], channels[b]
        fill(
            act_scrs[b], 0, b, dims,
            lambda r: jnp.maximum(x_refs[b][r].astype(F32), 0.0), top, bot, left, right,
        )
        fill(
            grad_scrs[b], 1, b, dims,
            lambda r: sc_refs[b][r].astype(F32), top, bot, left, right,
        )
        resp = jnp.zeros((h * w, c), F32)
        adj = jnp.zeros((h * w, c), F32)
        for q in range(3):
            rows = shifted(act_scrs[b], h, w, q)
            grads = shifted(grad_scrs[b], h, w, 2 - q)
            for p in range(3):
                k = k_refs[b][p, q]
                resp = resp + dot(stack(rows[p : p + h]), k, 1, 1)
                adj = adj + dot(stack(grads[2 - p : 2 - p + h]), k)
        gain = g_refs[b][...]
        unit, back = [], []
        for r in range(h):
            x = x_refs[b][r].astype(F32)
            unit.append((x + gain * resp[r * w : (r + 1) * w]).astype(BF))
            back.append(up_refs[b][r] + jnp.where(x > 0, adj[r * w : (r + 1) * w], 0.0))
        units.append(unit)
        emit(b, back_refs[b], back)
    mixers = [f_refs[j][...] for j in range(4)]

    def mix(v, j, i):
        off = source_offset(channels, j, i)
        if j == 3:
            return dot(v, mixers[3][off : off + channels[i]])
        return dot(v, mixers[j][:, off : off + channels[i]], 1, 1)

    sums = [[u.astype(F32) for u in units[j]] for j in range(4)]
    for i in range(4):
        for j in range(i + 1, 4):
            f = 2 ** (j - i)
            pool = group_matrix(widths[j], widths[i], f)
            for r in range(heights[j]):
                s = dot(pool, units[i][r * f])
                for k in range(1, f):
                    s = s + dot(pool, units[i][r * f + k])
                s = (s * (1.0 / (f * f))).astype(BF)
                sums[j][r] = sums[j][r] + mix(s, j, i)
        for j in range(i):
            f = 2 ** (i - j)
            spread = group_matrix(widths[i], widths[j], f, True)
            for r in range(heights[i]):
                v = mix(dot(spread, units[i][r]).astype(BF), j, i)
                for k in range(f):
                    sums[j][r * f + k] = sums[j][r * f + k] + v
    for j in range(4):
        emit(j, merged_refs[j], sums[j])


def gather_positions(n_branch, n_chip):
    return [(m, l, k) for m in range(2) for l in range(n_branch) for k in range(n_chip)]


def finish_kernel(dims, n_branch, n_chip, scales, *refs):
    heights, widths, channels = dims
    idx, own, other = refs[0], refs[1], refs[2]
    outs = refs[3:7]
    flat, act, scl, acc = refs[7:11]
    size = flat.shape[1]
    c0, c1, c2, c3 = channels
    w3 = widths[3]
    rows, cols = 2 * n_chip, n_branch * w3
    core, branch, chip = idx[0], idx[1], idx[2]
    act[0] = jnp.zeros(act.shape[1:], F32)
    act[rows + 1] = jnp.zeros(act.shape[1:], F32)
    for r in range(rows):
        act[r + 1, 0:LEFT, :] = jnp.zeros((LEFT, c3), F32)
        act[r + 1, LEFT + cols :, :] = jnp.zeros((8, c3), F32)
    for m, l, k in gather_positions(n_branch, n_chip):
        src = own if m == 0 else other
        c = (core + m) % 2
        b = (branch + l) % n_branch
        z = (chip + k) % n_chip
        piece = (c * n_branch + b) * n_chip + z
        flat[piece] = src[l, k, 0:size, :]
        r = z * 2 + c
        off = pl.multiple_of(b * w3, w3)
        for t in range(3):
            at = size + t * w3
            act[r + 1, pl.ds(LEFT + off, w3), t * 128 : (t + 1) * 128] = src[
                l, k, at : at + w3, :
            ].astype(F32)
            at = size + (3 + t) * w3
            scl[r, pl.ds(off, w3), t * 128 : (t + 1) * 128] = src[l, k, at : at + w3, :]
    full = flat[...].astype(F32).reshape(flat.shape[0] * size, 128)
    base1 = 9 * c2 * 3 // 2
    base0 = base1 + 9 * c1
    half = c2 // 2
    for tap in range(9):
        p, q = tap // 3, tap % 3
        outs[2][p, q, :, 0:128] = (full[tap * c2 : (tap + 1) * c2] * scales[2]).astype(BF)
        at = 9 * c2 + tap * half
        both = full[at : at + half]
        tail = jnp.concatenate([both[:, :64], both[:, 64:]], axis=0)
        outs[2][p, q, :, 128:c2] = (tail * scales[2]).astype(BF)
        at = base1 + tap * c1
        outs[1][p, q] = (full[at : at + c1, :c1] * scales[1]).astype(BF)
        at = base0 + (tap // 2) * c0
        lane = 64 * (tap % 2)
        outs[0][p, q] = (full[at : at + c0, lane : lane + c0] * scales[0]).astype(BF)
    for q in range(3):
        for p in range(3):
            acc[...] = jnp.zeros(acc.shape, F32)
            step = 4 if rows % 4 == 0 else 2

            @pl.loop(0, rows // step)
            def _(t, p=p, q=q, step=step):
                win = jnp.concatenate(
                    [
                        act[t * step + s + p, LEFT - 1 + q : LEFT - 1 + q + cols, :].astype(BF)
                        for s in range(step)
                    ],
                    axis=0,
                )
                grad = jnp.concatenate([scl[t * step + s] for s in range(step)], axis=0)
                acc[...] += dot(grad, win, 0, 0)

            outs[3][p, q] = (acc[...] * scales[3]).astype(BF)


def local(*args):
    maps, kernels, gains, mixers, cotans = (args[4 * k : 4 * k + 4] for k in range(5))
    n_rows, n_branch = lax.axis_size("rows"), lax.axis_size("branch")
    n_chip = n_rows // 2
    channels = [a.shape[0] for a in maps]
    heights = [a.shape[1] for a in maps]
    widths = [a.shape[2] for a in maps]
    dims = (heights, widths, channels)
    last = lambda a: jnp.transpose(a, (1, 2, 0))
    xs = [maps[0], maps[1], last(maps[2]), last(maps[3])]
    ds = [cotans[0], cotans[1], last(cotans[2]), last(cotans[3])]
    gs = [g.reshape(1, -1) for g in gains]
    fs = [mixers[0], mixers[1], mixers[2], mixers[3].T]
    shapes = [(heights[b], widths[b], channels[b]) for b in range(4)]
    edge = sds((2, 144, PACK), BF)
    side = sds((2, 16, PACK), BF)
    outs = call(
        functools.partial(upstream_kernel, dims),
        [sds(shapes[0], BF), sds(shapes[1], BF)]
        + [sds(s, F32) for s in shapes]
        + [sds(s, BF) for s in shapes]
        + [edge, edge, side, side],
        xs + ds + gs + fs,
    )
    xt = [outs[0], outs[1], xs[2], xs[3]]
    ups, scs = outs[2:6], outs[6:10]
    top, bot, left, right = outs[10:14]
    down = [(i, i + 1) for i in range(n_rows - 1)]
    rise = [(i + 1, i) for i in range(n_rows - 1)]
    from_top = lax.ppermute(bot, "rows", down)
    from_bot = lax.ppermute(top, "rows", rise)
    left = jnp.concatenate([left, from_top[:, 128:136], from_bot[:, 128:136]], axis=1)
    right = jnp.concatenate([right, from_top[:, 136:144], from_bot[:, 136:144]], axis=1)
    ahead = [(i, i + 1) for i in range(n_branch - 1)]
    behind = [(i + 1, i) for i in range(n_branch - 1)]
    from_left = lax.ppermute(right, "branch", ahead)
    from_right = lax.ppermute(left, "branch", behind)
    edges = [from_top, from_bot, from_left, from_right]

    pad = lambda b: pltpu.VMEM((heights[b] + 2, widths[b] + 16, channels[b]), F32)
    pieces = 2 * n_branch * n_chip
    packed_rows = 9 * (channels[2] * 3 // 2 + channels[1]) + 5 * channels[0]
    size = -(-packed_rows // (8 * pieces)) * 8
    (partial,) = call(
        functools.partial(weight_grads_kernel, dims),
        [sds((pieces * size, 128), BF)],
        xt[:3] + list(scs[:3]) + edges,
        [pad(0), pad(1), pad(2)],
    )
    row_id = lax.axis_index("rows")
    core, chip, branch = row_id % 2, row_id // 2, lax.axis_index("branch")

    def reduce_stage(values, axis, n, me, pairs):
        own = lax.dynamic_index_in_dim(values, me, 0, False)
        got = [
            lax.ppermute(lax.dynamic_index_in_dim(values, (me + k) % n, 0, False), axis, pairs(k))
            for k in range(1, n)
        ]
        out = own.astype(F32)
        for g in got:
            out = out + g.astype(F32)
        return out.astype(BF)

    swap = lambda k: [(i, i ^ 1) for i in range(n_rows)]
    around = lambda k: [(i, (i + k) % n_branch) for i in range(n_branch)]
    along = lambda k: [(i, (i + 2 * k) % n_rows) for i in range(n_rows)]
    part = partial.reshape(2, n_branch, n_chip, -1, 128)
    part = reduce_stage(part, "rows", 2, core, swap)
    part = reduce_stage(part, "branch", n_branch, branch, around)
    part = reduce_stage(part, "rows", n_chip, chip, along)

    act32 = jnp.maximum(xt[3], jnp.zeros((), BF)).reshape(widths[3], channels[3])
    lanes = lambda a: [a[:, k * 128 : (k + 1) * 128] for k in range(channels[3] // 128)]
    mine = jnp.concatenate(
        [part] + lanes(act32) + lanes(scs[3].reshape(widths[3], channels[3])), axis=0
    )

    def gather_stage(values, axis, n, pairs):
        back = lambda k: [(t, s) for s, t in pairs(k)]
        return jnp.stack([values] + [lax.ppermute(values, axis, back(k)) for k in range(1, n)])

    got = gather_stage(mine, "rows", n_chip, along)
    got = gather_stage(got, "branch", n_branch, around)
    other = lax.ppermute(got, "rows", swap(1))

    merged_back = call(
        functools.partial(maps_kernel, dims),
        [sds(maps[0].shape, BF), sds(maps[1].shape, BF), sds(shapes[2], BF), sds(shapes[3], BF)] * 2,
        xt + list(scs) + list(ups) + gs + fs + list(kernels) + edges,
        [pad(b) for b in range(4)] * 2
        + [pltpu.VMEM((heights[b], channels[b], widths[b]), F32) for b in range(4)],
    )
    scales = [
        1.0 / math.sqrt(heights[b] * n_rows * widths[b] * n_branch) for b in range(4)
    ]
    idx = jnp.stack([core, branch, chip]).astype(jnp.int32)
    cols = n_branch * widths[3]
    kgrads = pl.pallas_call(
        functools.partial(finish_kernel, dims, n_branch, n_chip, scales),
        out_shape=[sds(k.shape, BF) for k in kernels],
        in_specs=[pl.BlockSpec(memory_space=pltpu.SMEM)]
        + [pl.BlockSpec(memory_space=pltpu.VMEM)] * 2,
        out_specs=[pl.BlockSpec(memory_space=pltpu.VMEM)] * 4,
        scratch_shapes=[
            pltpu.VMEM((pieces, size, 128), BF),
            pltpu.VMEM((n_rows + 2, cols + 16, channels[3]), F32),
            pltpu.VMEM((n_rows, cols, channels[3]), BF),
            pltpu.VMEM((channels[3], channels[3]), F32),
        ],
        compiler_params=pltpu.CompilerParams(vmem_limit_bytes=60 * 1024 * 1024),
        cost_estimate=pl.CostEstimate(flops=3 * 10**9, bytes_accessed=10**7, transcendentals=0),
    )(idx, got, other)
    unlast = lambda a: jnp.transpose(a, (2, 0, 1))
    m, bk = merged_back[:4], merged_back[4:]
    return (
        m[0], m[1], unlast(m[2]), unlast(m[3]),
        bk[0], bk[1], unlast(bk[2]), unlast(bk[3]),
        *kgrads,
    )


def solution(mesh):
    maps = P(None, "rows", "branch")
    in_specs = (maps,) * 4 + (P(),) * 12 + (maps,) * 4
    out_specs = (maps,) * 8 + (P(),) * 4
    return jax.shard_map(
        lambda *args: local(*args),
        mesh=mesh, in_specs=in_specs, out_specs=out_specs, check_vma=False,
    )
```

```python
import functools
import math

import jax
import jax.numpy as jnp
from jax import lax
from jax.experimental import pallas as pl
from jax.experimental.pallas import tpu as pltpu
from jax.sharding import PartitionSpec as P

BF = jnp.bfloat16
F32 = jnp.float32
LEFT = 8
PACK = 384
WHOLE = 61
COARSE = 46


def dot(a, b, ca=1, cb=0):
    return lax.dot_general(a, b, (((ca,), (cb,)), ((), ())), preferred_element_type=F32)


def source_offset(channels, target, source):
    return sum(channels[k] for k in range(source) if k != target)


class Fetched:
    def __init__(self, ref, copy):
        self.ref, self.copy, self.shape = ref, copy, ref.shape
        copy.start()

    def wait(self):
        if self.copy is not None:
            self.copy.wait()
            self.copy = None

    def __getitem__(self, at):
        self.wait()
        return self.ref[at]


class Sent:
    def __init__(self, ref, copy):
        self.ref, self.copy, self.shape, self.started = ref, copy, ref.shape, False

    def __setitem__(self, at, value):
        self.ref[at] = value

    def __getitem__(self, at):
        return self.ref[at]

    def flush(self):
        if not self.started:
            self.copy.start()
            self.started = True

    def wait(self):
        self.flush()
        self.copy.wait()


def flush(*refs):
    for ref in refs:
        if isinstance(ref, Sent):
            ref.flush()


def call(body, outs, args, scratch=(), far=(), far_out=(), placed=False, deps=(), raw_out=(), flops=2 * 10**9, limit=24):
    far, far_out = list(far), list(far_out)
    n_in, n_out, n_far = len(args), len(outs), len(far)
    n_moved = n_far + len(far_out)

    def wrapped(*refs):
        row = lax.axis_index("rows")
        place = (row % 2, lax.axis_index("branch"), row // 2)
        ins, rest = list(refs[:n_in]), refs[n_in + len(deps) :]
        results, held, sems = list(rest[:n_out]), rest[n_out : n_out + n_moved], rest[-1]
        copy = lambda a, b, k: pltpu.make_async_copy(a, b, sems.at[k])
        for at, k in enumerate(far):
            ins[k] = Fetched(held[at], copy(ins[k], held[at], at))
        for at, k in enumerate(far_out, n_far):
            results[k] = Sent(held[at], copy(held[at], results[k], at))
        body(*([place] if placed else []), *ins, *results, *rest[n_out + n_moved : -1])
        for k in far_out:
            results[k].flush()
        for ref in [ins[k] for k in far] + [results[k] for k in far_out]:
            ref.wait()

    def space(k, kept):
        return pl.BlockSpec(memory_space=pl.ANY if k in kept else pltpu.VMEM)

    moved = [args[k] for k in far] + [outs[k] for k in far_out]
    return pl.pallas_call(
        wrapped,
        out_shape=outs,
        in_specs=[space(k, far) for k in range(n_in)]
        + [pl.BlockSpec(memory_space=pl.ANY) for _ in deps],
        out_specs=[space(k, far_out + list(raw_out)) for k in range(n_out)],
        scratch_shapes=[pltpu.VMEM(a.shape, a.dtype) for a in moved]
        + list(scratch)
        + [pltpu.SemaphoreType.DMA((max(n_moved, 1),))],
        compiler_params=pltpu.CompilerParams(vmem_limit_bytes=limit * 1024 * 1024),
        cost_estimate=pl.CostEstimate(flops=flops, bytes_accessed=10**6, transcendentals=0),
    )(*args, *deps)


def sds(shape, dtype):
    return jax.ShapeDtypeStruct(shape, dtype)


def group_matrix(groups, cells, factor, transposed=False):
    shape = (cells, groups) if transposed else (groups, cells)
    g = lax.broadcasted_iota(jnp.int32, shape, 1 if transposed else 0)
    c = lax.broadcasted_iota(jnp.int32, shape, 0 if transposed else 1)
    return jnp.where((c >= g * factor) & (c < g * factor + factor), 1.0, 0.0).astype(BF)


def row_pack(row, channels):
    blocks = PACK // channels
    part = row.shape[0] // blocks
    return jnp.concatenate([row[k * part : (k + 1) * part] for k in range(blocks)], axis=1)


def row_unpack(packed, channels):
    blocks = PACK // channels
    return jnp.concatenate(
        [packed[:, k * channels : (k + 1) * channels] for k in range(blocks)], axis=0
    )


def col_rows(heights):
    starts, at = [], 0
    for h in heights:
        starts.append(at)
        at += h
    return starts


def channels_last(ref, height, channels):
    eye = group_matrix(channels, channels, 1)
    rows = jnp.swapaxes(ref[...].astype(F32), 0, 1).astype(BF)
    return [dot(rows[r], eye, 0, 0).astype(BF) for r in range(height)]


def pack_edges(n, b, dims, rows, top, bot, left, right):
    heights, widths, channels = dims
    h, w, c = heights[b], widths[b], channels[b]
    start = col_rows(heights)[b]
    for out, row in ((top, rows[0]), (bot, rows[h - 1])):
        out[n, b * 32 : (b + 1) * 32, :] = row_pack(row, c).astype(BF)
        out[n, 128 + b : 129 + b, :c] = row[0:1].astype(BF)
        out[n, 136 + b : 137 + b, :c] = row[w - 1 : w].astype(BF)
    left[n, start : start + h, :c] = stack([row[0:1] for row in rows]).astype(BF)
    right[n, start : start + h, :c] = stack([row[w - 1 : w] for row in rows]).astype(BF)


def gain_row(ref):
    g = ref[...]
    return jnp.concatenate([g[k : k + 1] for k in range(g.shape[0])], axis=1)


def stack(rows):
    return rows[0] if len(rows) == 1 else jnp.concatenate(rows, axis=0)


def upstream_kernel(dims, idx, *refs):
    heights, widths, channels = dims
    d_refs, f_refs, g_refs, x_refs = refs[0:4], refs[4:8], refs[8:12], refs[12:16]
    xt, up_refs, sc_refs = refs[16:20], refs[20:24], refs[24:28]
    inner, outer, left, right, coarse, ends = refs[28:34]
    edges = [ends.at[0], ends.at[1], left, right]
    left[...] = jnp.zeros(left.shape, F32).astype(BF)
    right[...] = jnp.zeros(right.shape, F32).astype(BF)
    ends[:, :, 128:, :] = jnp.zeros((2, 2, 16, PACK), F32).astype(BF)
    dt = []
    for b in range(4):
        if b < 2:
            dt.append(channels_last(d_refs[b], heights[b], channels[b]))
        else:
            dt.append([d_refs[b][r] for r in range(heights[b])])
    mixers = [f_refs[j][...] for j in range(4)]

    def block(j, i):
        off = source_offset(channels, j, i)
        if j == 3:
            return mixers[3][off : off + channels[i]]
        return mixers[j][:, off : off + channels[i]]

    acc = [[dt[i][r].astype(F32) for r in range(heights[i])] for i in range(4)]
    for j in range(4):
        for i in range(j + 1, 4):
            f = 2 ** (i - j)
            pool = group_matrix(widths[i], widths[j], f)
            mat = block(j, i)
            for r in range(heights[i]):
                s = dot(pool, dt[j][r * f])
                for k in range(1, f):
                    s = s + dot(pool, dt[j][r * f + k])
                acc[i][r] = acc[i][r] + dot(s.astype(BF), mat)
        for i in range(j):
            f = 2 ** (j - i)
            spread = group_matrix(widths[j], widths[i], f, True)
            mat = block(j, i)
            for r in range(heights[j]):
                z = dot(spread, dt[j][r]).astype(BF)
                v = dot(z, mat, 1, 1) if j == 3 else dot(z, mat)
                v = v * (1.0 / (f * f))
                for k in range(f):
                    acc[i][r * f + k] = acc[i][r * f + k] + v
    for b in range(4):
        gain = gain_row(g_refs[b])
        scaled = []
        for r in range(heights[b]):
            Packed(up_refs[b], channels[b])[r] = acc[b][r]
            s = (gain * acc[b][r]).astype(BF)
            Packed(sc_refs[b], channels[b])[r] = s
            scaled.append(s.astype(F32))
        flush(up_refs[b], sc_refs[b])
        pack_edges(1, b, dims, scaled, *edges)
        if b < 2:
            rows = channels_last(x_refs[b], heights[b], channels[b])
        else:
            rows = [x_refs[b][r] for r in range(heights[b])]
        for r in range(heights[b]):
            Packed(xt[b], channels[b])[r] = rows[r]
        flush(xt[b])
        pack_edges(0, b, dims, [jnp.maximum(v.astype(F32), 0.0) for v in rows], *edges)
    inner[...] = ends[1 - idx[0]]
    outer[...] = ends[idx[0]]
    w3 = widths[3]
    for r in range(heights[3]):
        coarse[0, r * w3 : (r + 1) * w3] = jnp.maximum(x_refs[3][r].astype(F32), 0.0).astype(BF)
        coarse[1, r * w3 : (r + 1) * w3] = sc_refs[3][r]


class Packed:
    def __init__(self, ref, channels):
        self.ref, self.c, self.two = ref, channels, channels <= 64

    def __getitem__(self, r):
        row = self.ref[r]
        if self.two:
            row = jnp.concatenate([row[:, : self.c], row[:, 64 : 64 + self.c]], axis=0)
        return row

    def __setitem__(self, r, row):
        row = row.astype(F32)
        if self.two:
            half = row.shape[0] // 2
            gap = jnp.zeros((half, 64 - self.c), F32)
            row = jnp.concatenate([row[:half], gap, row[half:], gap], axis=1)
        self.ref[r] = row.astype(BF)


def packed(dims, refs):
    return [Packed(ref, c) for ref, c in zip(refs, dims[2])]


def pick(odd, first, second):
    return jnp.where(odd == 0, first.astype(F32), second.astype(F32))


def fill(scr, n, b, dims, interior, idx, in_row, out_row, in_col, out_col):
    heights, widths, channels = dims
    h, w, c = heights[b], widths[b], channels[b]
    start = col_rows(heights)[b]
    for r in range(h):
        scr[r + 1, LEFT : LEFT + w, :] = interior(r)
    lines = slice(b * 32, (b + 1) * 32)
    core, band = idx[0], idx[1] % 2
    for first, second, at in ((out_row, in_row, 0), (in_row, out_row, h + 1)):
        packed = pick(core, first[n, lines, :], second[n, lines, :])
        scr[at, LEFT : LEFT + w, :] = row_unpack(packed, c)
    for first, second, at in ((out_col, in_col, LEFT - 1), (in_col, out_col, LEFT + w)):
        vals = pick(band, first[n], second[n])
        for r in range(h):
            scr[r + 1, at : at + 1, :] = vals[start + r : start + r + 1, :c]
        scr[0, at : at + 1, :] = vals[16 + b : 17 + b, :c]
        scr[h + 1, at : at + 1, :] = vals[24 + b : 25 + b, :c]


def shifted(scr, h, w, q):
    return [scr[r, LEFT - 1 + q : LEFT - 1 + q + w, :].astype(BF) for r in range(h + 2)]


def side_by_side(scr, h, w, order):
    gap = jnp.zeros((w, 64 - scr.shape[2]), F32)
    rows = []
    for r in range(h + 2):
        parts = []
        for q in order:
            parts += [scr[r, LEFT - 1 + q : LEFT - 1 + q + w, :], gap]
        rows.append(jnp.concatenate(parts, axis=1).astype(BF))
    return rows


def apart(blocks, axis):
    parts = []
    for block in blocks:
        shape = list(block.shape)
        shape[axis] = 64 - shape[axis]
        parts += [block.astype(F32), jnp.zeros(shape, F32)]
    return jnp.concatenate(parts, axis=axis).astype(BF)


def forward_taps(scr, kernel, h, w):
    if scr.shape[2] <= 64:
        rows = side_by_side(scr, h, w, range(3))
        return sum(
            dot(stack(rows[p : p + h]), apart([kernel[p, q] for q in range(3)], 1), 1, 1)
            for p in range(3)
        )
    total = 0
    for q in range(3):
        rows = shifted(scr, h, w, q)
        total = total + sum(dot(stack(rows[p : p + h]), kernel[p, q], 1, 1) for p in range(3))
    return total


def adjoint_taps(scr, kernel, h, w):
    if scr.shape[2] <= 64:
        rows = side_by_side(scr, h, w, (2, 1, 0))
        return sum(
            dot(stack(rows[2 - p : 2 - p + h]), apart([kernel[p, q] for q in range(3)], 0))
            for p in range(3)
        )
    total = 0
    for q in range(3):
        rows = shifted(scr, h, w, 2 - q)
        total = total + sum(dot(stack(rows[2 - p : 2 - p + h]), kernel[p, q]) for p in range(3))
    return total


def weight_grads_kernel(dims, *refs):
    heights, widths, channels = dims
    idx, x_refs, sc_refs = refs[0], packed(dims, refs[1:4]), packed(dims, refs[4:7])
    edges = refs[7:11]
    keep, send, out, *scrs = refs[11:]
    c0, c1, c2 = channels[0], channels[1], channels[2]
    for b in (2, 1, 0):
        h, w, c = heights[b], widths[b], channels[b]
        fill(scrs[b], 0, b, dims, lambda r: jnp.maximum(x_refs[b][r].astype(F32), 0.0), idx, *edges)
        s_all = stack([sc_refs[b][r] for r in range(h)])
        if c <= 64:
            rows = side_by_side(scrs[b], h, w, range(3))
            wide = [dot(s_all, stack(rows[p : p + h]), 0, 0) for p in range(3)]
        for q in range(3):
            if c > 64:
                rows = shifted(scrs[b], h, w, q)
            for p in range(3):
                if c > 64:
                    g = dot(s_all, stack(rows[p : p + h]), 0, 0)
                else:
                    g = wide[p][:, 64 * q : 64 * q + c]
                tap = p * 3 + q
                if b == 2:
                    out[tap * c2 : (tap + 1) * c2, :] = g[:, :128].astype(BF)
                    half = c2 // 2
                    at = 9 * c2 + tap * half
                    both = jnp.concatenate([g[:half, 128:], g[half:, 128:]], axis=1)
                    out[at : at + half, :] = both.astype(BF)
                elif b == 1:
                    at = 9 * c2 * 3 // 2 + tap * c1
                    out[at : at + c1, :c1] = g.astype(BF)
                else:
                    at = 9 * c2 * 3 // 2 + 9 * c1 + (tap // 2) * c0
                    lane = 64 * (tap % 2)
                    out[at : at + c0, lane : lane + c0] = g.astype(BF)
    half = keep.shape[0]
    keep[...] = out[pl.ds(pl.multiple_of(idx[0] * half, 16), half), :]
    send[...] = out[pl.ds(pl.multiple_of((1 - idx[0]) * half, 16), half), :]


def pair_sum_kernel(n_branch, idx, keep, got, coarse, *outs):
    size = outs[0].shape[0]
    for k in range(n_branch):
        at = pl.ds(pl.multiple_of((idx[1] + k) % n_branch * size, 16), size)
        outs[k][...] = (keep[at, :].astype(F32) + got[at, :].astype(F32)).astype(BF)
    outs[-1][...] = coarse[...]


def stack_kernel(count, *refs):
    for k in range(count):
        refs[-1][k] = refs[k][...]


def corner_kernel(idx, left, right, in_row, out_row, inner, outer):
    core, band = idx[0], idx[1] % 2
    cols = []
    for side, at in ((left, 128), (right, 136)):
        in_part, out_part = in_row[:, at : at + 8, :], out_row[:, at : at + 8, :]
        above, below = pick(core, out_part, in_part), pick(core, in_part, out_part)
        cols.append(jnp.concatenate([side[...].astype(F32), above, below], axis=1))
    inner[...] = pick(band, cols[1], cols[0]).astype(BF)
    outer[...] = pick(band, cols[0], cols[1]).astype(BF)


def sum_kernel(count, *refs):
    total = refs[0][...].astype(F32)
    for k in range(1, count):
        total = total + refs[k][...].astype(F32)
    refs[-1][...] = total.astype(BF)


def ordered_sum_kernel(n, idx, *refs):
    held = refs[-1]
    for k in range(n):
        held[(idx[2] + k) % n] = refs[k][...]
    total = held[0].astype(F32)
    for k in range(1, n):
        total = total + held[k].astype(F32)
    refs[n][...] = total.astype(BF)


def forward_kernel(dims, idx, *refs):
    heights, widths, channels = dims
    x_refs = packed(dims, refs[0:4])
    g_refs, f_refs, k_refs = refs[4:8], refs[8:12], refs[12:16]
    edges = refs[16:20]
    refs = refs[20:]
    merged_refs, scrs, wide = refs[0:4], refs[4:8], refs[8:12]
    units = []
    for b in range(4):
        h, w, c = heights[b], widths[b], channels[b]
        fill(scrs[b], 0, b, dims, lambda r: jnp.maximum(x_refs[b][r].astype(F32), 0.0), idx, *edges)
        resp = forward_taps(scrs[b], k_refs[b], h, w)
        gain = gain_row(g_refs[b])
        units.append(
            [
                (x_refs[b][r].astype(F32) + gain * resp[r * w : (r + 1) * w]).astype(BF)
                for r in range(h)
            ]
        )
    mixers = [f_refs[j][...] for j in range(4)]

    def mix(v, j, i):
        off = source_offset(channels, j, i)
        if j == 3:
            return dot(v, mixers[3][off : off + channels[i]])
        return dot(v, mixers[j][:, off : off + channels[i]], 1, 1)

    sums = [[u.astype(F32) for u in units[j]] for j in range(4)]
    for i in range(4):
        for j in range(i + 1, 4):
            f = 2 ** (j - i)
            pool = group_matrix(widths[j], widths[i], f)
            for r in range(heights[j]):
                s = dot(pool, units[i][r * f])
                for k in range(1, f):
                    s = s + dot(pool, units[i][r * f + k])
                s = (s * (1.0 / (f * f))).astype(BF)
                sums[j][r] = sums[j][r] + mix(s, j, i)
        for j in range(i):
            f = 2 ** (i - j)
            spread = group_matrix(widths[i], widths[j], f, True)
            for r in range(heights[i]):
                v = mix(dot(spread, units[i][r]).astype(BF), j, i)
                for k in range(f):
                    sums[j][r * f + k] = sums[j][r * f + k] + v
    for j in range(4):
        emit(j, heights, merged_refs[j], sums[j], wide[j])


def emit(b, heights, out, rows, stage):
    if b >= 2:
        for r in range(heights[b]):
            out[r] = rows[r].astype(BF)
        flush(out)
        return
    for r in range(heights[b]):
        stage[r] = rows[r].T
    out[...] = jnp.swapaxes(stage[...], 0, 1).astype(BF)
    flush(out)


def adjoint_kernel(dims, idx, *refs):
    heights, widths, channels = dims
    x_refs, sc_refs, up_refs = (packed(dims, refs[k : k + 4]) for k in (0, 4, 8))
    k_refs = refs[12:16]
    edges = refs[16:20]
    refs = refs[20:]
    back_refs, scrs, wide = refs[0:4], refs[4:8], refs[8:12]
    for b in range(4):
        h, w, c = heights[b], widths[b], channels[b]
        fill(scrs[b], 1, b, dims, lambda r: sc_refs[b][r].astype(F32), idx, *edges)
        adj = adjoint_taps(scrs[b], k_refs[b], h, w)
        back = [
            up_refs[b][r].astype(F32)
            + jnp.where(x_refs[b][r].astype(F32) > 0, adj[r * w : (r + 1) * w], 0.0)
            for r in range(h)
        ]
        emit(b, heights, back_refs[b], back, wide[b])


def coarse_kernel(dims, n_branch, n_chip, scale, idx, *refs):
    out, act, win, grad, acc, taps, sems = refs[-7:]
    w3, c3 = dims[1][3], dims[2][3]
    rows, cols = 2 * n_chip, n_branch * w3
    act[0] = jnp.zeros(act.shape[1:], F32)
    act[rows + 1] = jnp.zeros(act.shape[1:], F32)
    for r in range(rows):
        act[r + 1, 0:LEFT, :] = jnp.zeros((LEFT, c3), F32)
        act[r + 1, LEFT + cols :, :] = jnp.zeros((8, c3), F32)
    for m in range(2):
        for l in range(n_branch):
            for k in range(n_chip):
                src = refs[m * n_branch + l]
                r = (idx[2] + k) % n_chip * 2 + (idx[0] + m) % 2
                off = pl.multiple_of((idx[1] + l) % n_branch * w3, w3)
                act[r + 1, pl.ds(LEFT + off, w3), :] = src[k, 0].astype(F32)
                win[r, pl.ds(off, w3), :] = src[k, 1]
    for r in range(rows):
        grad[:, r * cols : (r + 1) * cols] = win[r].astype(F32).T.astype(BF)
    span = rows * cols
    step = min(span, 1024)
    copies = []
    for q in range(3):
        for r in range(rows + 2):
            win[r] = act[r, LEFT - 1 + q : LEFT - 1 + q + cols, :].astype(BF)
        for p in range(3):
            if step == span:
                total = dot(grad[...], win[p : p + rows].reshape(span, c3))
            else:
                acc[...] = jnp.zeros(acc.shape, F32)
                lines = step // cols

                @pl.loop(0, rows // lines)
                def _(t, p=p):
                    some = win[pl.ds(t * lines + p, lines)].reshape(step, c3)
                    acc[...] += dot(grad[:, pl.ds(pl.multiple_of(t * step, step), step)], some)

                total = acc[...]
            taps[p, q] = (total * scale).astype(BF)
            copies.append(pltpu.make_async_copy(taps.at[p, q], out.at[p, q], sems.at[p, q]))
            copies[-1].start()
    for copy in copies:
        copy.wait()


def finish_kernel(dims, n_branch, scales, idx, *refs):
    channels = dims[2]
    parts = refs[: 2 * n_branch]
    outs, flat = refs[-4:-1], refs[-1]
    c0, c1, c2 = channels[0], channels[1], channels[2]
    size = parts[0].shape[0]
    for k, part in enumerate(parts):
        core, band = (idx[0] + k // n_branch) % 2, (idx[1] + k) % n_branch
        at = pl.multiple_of((core * n_branch + band) * size, 16)
        flat[pl.ds(at, size), :] = part[...].astype(F32)
    base1 = 9 * c2 * 3 // 2
    base0 = base1 + 9 * c1
    half = c2 // 2
    for tap in range(9):
        p, q = tap // 3, tap % 3
        outs[2][p, q, :, 0:128] = (flat[tap * c2 : (tap + 1) * c2, :] * scales[2]).astype(BF)
        at = 9 * c2 + tap * half
        both = flat[at : at + half, :]
        tail = jnp.concatenate([both[:, :64], both[:, 64:]], axis=0)
        outs[2][p, q, :, 128:c2] = (tail * scales[2]).astype(BF)
        at = base1 + tap * c1
        outs[1][p, q] = (flat[at : at + c1, :c1] * scales[1]).astype(BF)
        at = base0 + (tap // 2) * c0
        lane = 64 * (tap % 2)
        outs[0][p, q] = (flat[at : at + c0, lane : lane + c0] * scales[0]).astype(BF)


def local(*args):
    maps, kernels, gains, mixers, cotans = (args[4 * k : 4 * k + 4] for k in range(5))
    n_rows, n_branch = lax.axis_size("rows"), lax.axis_size("branch")
    n_chip = n_rows // 2
    channels = [a.shape[0] for a in maps]
    heights = [a.shape[1] for a in maps]
    widths = [a.shape[2] for a in maps]
    dims = (heights, widths, channels)
    last = lambda a: jnp.transpose(a, (1, 2, 0))
    unlast = lambda a: jnp.transpose(a, (2, 0, 1))
    xs = [maps[0], maps[1], last(maps[2]), last(maps[3])]
    ds = [cotans[0], cotans[1], last(cotans[2]), last(cotans[3])]
    gs = [g.reshape(-1, 128) if g.shape[0] % 128 == 0 else g.reshape(1, -1) for g in gains]
    fs = [mixers[0], mixers[1], mixers[2], mixers[3].T]
    shapes = [(heights[b], widths[b], channels[b]) for b in range(4)]
    kept = [sds((h, w // 2, 128) if c <= 64 else (h, w, c), BF) for h, w, c in shapes]
    scales = [1.0 / math.sqrt(heights[b] * n_rows * widths[b] * n_branch) for b in range(4)]
    swap = lambda n: [(i, i ^ 1) for i in range(n)]
    hop = lambda n: [(i, i + 1 if i % 2 else i - 1) for i in range(1, n - 1)]
    core_swap = lambda a: lax.ppermute(a, "rows", swap(n_rows))
    from_branch = lambda k: [((i + k) % n_branch, i) for i in range(n_branch)]
    to_branch = lambda k: [(i, (i + k) % n_branch) for i in range(n_branch)]
    from_chip = lambda k: [((i + 2 * k) % n_rows, i) for i in range(n_rows)]

    outs = call(
        functools.partial(upstream_kernel, dims),
        kept * 3 + [sds((2, 144, PACK), BF)] * 2 + [sds((2, 16, PACK), BF)] * 2
        + [sds((2, heights[3] * widths[3], channels[3]), BF)],
        ds + fs + gs + xs,
        [pltpu.VMEM((2, 2, 144, PACK), BF)],
        placed=True, far=range(16), far_out=range(17), limit=WHOLE, flops=6 * 10**9,
    )
    xt, ups, scs = outs[:4], outs[4:8], outs[8:12]
    inner, outer, left, right, coarse = outs[12:]
    out_row = lax.ppermute(outer, "rows", hop(n_rows))
    in_row = core_swap(inner)
    inner, outer = call(
        corner_kernel, [sds((2, 32, PACK), BF)] * 2, [left, right, in_row, out_row],
        placed=True, far=range(4), far_out=range(2), limit=WHOLE,
    )
    out_col = lax.ppermute(outer, "branch", hop(n_branch))
    in_col = lax.ppermute(inner, "branch", swap(n_branch))
    edges = [in_row, out_row, in_col, out_col]

    pad = lambda b: pltpu.VMEM((heights[b] + 2, widths[b] + 16, channels[b]), F32)
    wide = [pltpu.VMEM((heights[b], channels[b], widths[b]), F32) for b in range(4)]
    pieces = 2 * n_branch
    packed_rows = 9 * (channels[2] * 3 // 2 + channels[1]) + 5 * channels[0]
    size = -(-packed_rows // (16 * pieces)) * 16
    part = sds((size, 128), BF)
    keep, send = call(
        functools.partial(weight_grads_kernel, dims),
        [sds((n_branch * size, 128), BF)] * 2,
        list(xt[:3]) + list(scs[:3]) + edges,
        [pltpu.VMEM((pieces * size, 128), BF), pad(0), pad(1), pad(2)],
        placed=True, far=(2, 5, 6, 7, 8, 9, 1, 4, 0, 3), far_out=(0, 1), limit=WHOLE, flops=4 * 10**9,
    )
    *parts, coarse = call(
        functools.partial(pair_sum_kernel, n_branch),
        [part] * n_branch + [sds(coarse.shape, BF)],
        [keep, core_swap(send), coarse],
        placed=True, far=range(3), far_out=range(n_branch + 1), limit=WHOLE,
    )
    got = [lax.ppermute(parts[k], "branch", to_branch(k)) for k in range(1, n_branch)]
    held = [coarse] + [lax.ppermute(coarse, "rows", from_chip(k)) for k in range(1, n_chip)]
    (held,) = call(
        functools.partial(stack_kernel, n_chip), [sds((n_chip,) + coarse.shape, BF)], held,
    )
    (part_sum,) = call(
        functools.partial(sum_kernel, n_branch), [part], [parts[0]] + got, deps=(held,)
    )
    got = [lax.ppermute(part_sum, "rows", from_chip(k)) for k in range(1, n_chip)]
    held = [held] + [lax.ppermute(held, "branch", from_branch(k)) for k in range(1, n_branch)]
    merged = call(
        functools.partial(forward_kernel, dims),
        [sds(maps[0].shape, BF), sds(maps[1].shape, BF), sds(shapes[2], BF), sds(shapes[3], BF)],
        list(xt) + gs + fs + list(kernels) + edges,
        [pad(b) for b in range(4)] + wide,
        placed=True, far_out=range(4), deps=(part_sum,), flops=6 * 10**9,
    )
    back = call(
        functools.partial(adjoint_kernel, dims),
        [sds(maps[0].shape, BF), sds(maps[1].shape, BF), sds(shapes[2], BF), sds(shapes[3], BF)],
        list(xt) + list(scs) + list(ups) + list(kernels) + edges,
        [pad(b) for b in range(4)] + wide,
        placed=True, far_out=range(4), deps=(part_sum,),
    )
    (total,) = call(
        functools.partial(ordered_sum_kernel, n_chip), [part], [part_sum] + got,
        [pltpu.VMEM((n_chip, size, 128), BF)], placed=True, deps=(merged[3], *held[1:]),
    )
    mine = [total] + [lax.ppermute(total, "branch", from_branch(k)) for k in range(1, n_branch)]
    held = held + [core_swap(a) for a in held]
    cols = n_branch * widths[3]
    (kgrad3,) = call(
        functools.partial(coarse_kernel, dims, n_branch, n_chip, scales[3]),
        [sds(kernels[3].shape, BF)],
        held,
        [
            pltpu.VMEM((n_rows + 2, cols + 16, channels[3]), F32),
            pltpu.VMEM((n_rows + 2, cols, channels[3]), BF),
            pltpu.VMEM((channels[3], n_rows * cols), BF),
            pltpu.VMEM((channels[3], channels[3]), F32),
            pltpu.VMEM(kernels[3].shape, BF),
            pltpu.SemaphoreType.DMA((3, 3)),
        ],
        placed=True, raw_out=(0,), deps=(total,), flops=5 * 10**9, limit=COARSE,
    )
    mine = mine + [core_swap(a) for a in mine]
    kgrads = call(
        functools.partial(finish_kernel, dims, n_branch, scales),
        [sds(k.shape, BF) for k in kernels[:3]],
        mine,
        [pltpu.VMEM((pieces * size, 128), F32)], placed=True, far_out=range(3), deps=(kgrad3, back[3]),
    )
    return (
        merged[0], merged[1], unlast(merged[2]), unlast(merged[3]),
        back[0], back[1], unlast(back[2]), unlast(back[3]),
        *kgrads, kgrad3,
    )


def solution(mesh):
    maps = P(None, "rows", "branch")
    in_specs = (maps,) * 4 + (P(),) * 12 + (maps,) * 4
    out_specs = (maps,) * 8 + (P(),) * 4
    return jax.shard_map(
        lambda *args: local(*args),
        mesh=mesh, in_specs=in_specs, out_specs=out_specs, check_vma=False,
    )
```

```python
import functools
import math

import jax
import jax.numpy as jnp
from jax import lax
from jax.experimental import pallas as pl
from jax.experimental.pallas import tpu as pltpu
from jax.sharding import PartitionSpec as P

BF = jnp.bfloat16
F32 = jnp.float32
LEFT = 8
PACK = 384
WHOLE = 61
COARSE = 46


def dot(a, b, ca=1, cb=0):
    return lax.dot_general(a, b, (((ca,), (cb,)), ((), ())), preferred_element_type=F32)


def source_offset(channels, target, source):
    return sum(channels[k] for k in range(source) if k != target)


class Fetched:
    def __init__(self, ref, copy):
        self.ref, self.copy, self.shape = ref, copy, ref.shape
        copy.start()

    def wait(self):
        if self.copy is not None:
            self.copy.wait()
            self.copy = None

    def __getitem__(self, at):
        self.wait()
        return self.ref[at]


class Sent:
    def __init__(self, ref, copy):
        self.ref, self.copy, self.shape, self.started = ref, copy, ref.shape, False

    def __setitem__(self, at, value):
        self.ref[at] = value

    def __getitem__(self, at):
        return self.ref[at]

    def flush(self):
        if not self.started:
            self.copy.start()
            self.started = True

    def wait(self):
        self.flush()
        self.copy.wait()


def flush(*refs):
    for ref in refs:
        if isinstance(ref, Sent):
            ref.flush()


def call(body, outs, args, scratch=(), far=(), far_out=(), placed=False, deps=(), raw_out=(), token=False, flops=2 * 10**9, limit=24):
    far, far_out = list(far), list(far_out)
    if token:
        outs = [*outs, sds((8, 128), F32)]
    n_in, n_out, n_far = len(args), len(outs), len(far)
    n_moved = n_far + len(far_out)

    def wrapped(*refs):
        row = lax.axis_index("rows")
        place = (row % 2, lax.axis_index("branch"), row // 2)
        ins, rest = list(refs[:n_in]), refs[n_in + len(deps) :]
        results, held, sems = list(rest[:n_out]), rest[n_out : n_out + n_moved], rest[-1]
        copy = lambda a, b, k: pltpu.make_async_copy(a, b, sems.at[k])
        for at, k in enumerate(far):
            ins[k] = Fetched(held[at], copy(ins[k], held[at], at))
        for at, k in enumerate(far_out, n_far):
            results[k] = Sent(held[at], copy(held[at], results[k], at))
        if token:
            results.pop()[...] = jnp.zeros((8, 128), F32)
        body(*([place] if placed else []), *ins, *results, *rest[n_out + n_moved : -1])
        for k in far_out:
            results[k].flush()
        for ref in [ins[k] for k in far] + [results[k] for k in far_out]:
            ref.wait()

    def space(k, kept):
        return pl.BlockSpec(memory_space=pl.ANY if k in kept else pltpu.VMEM)

    moved = [args[k] for k in far] + [outs[k] for k in far_out]
    return pl.pallas_call(
        wrapped,
        out_shape=outs,
        in_specs=[space(k, far) for k in range(n_in)]
        + [pl.BlockSpec(memory_space=pl.ANY) for _ in deps],
        out_specs=[space(k, far_out + list(raw_out)) for k in range(n_out)],
        scratch_shapes=[pltpu.VMEM(a.shape, a.dtype) for a in moved]
        + list(scratch)
        + [pltpu.SemaphoreType.DMA((max(n_moved, 1),))],
        compiler_params=pltpu.CompilerParams(vmem_limit_bytes=limit * 1024 * 1024),
        cost_estimate=pl.CostEstimate(flops=flops, bytes_accessed=10**6, transcendentals=0),
    )(*args, *deps)


def sds(shape, dtype):
    return jax.ShapeDtypeStruct(shape, dtype)


def group_matrix(groups, cells, factor, transposed=False):
    shape = (cells, groups) if transposed else (groups, cells)
    g = lax.broadcasted_iota(jnp.int32, shape, 1 if transposed else 0)
    c = lax.broadcasted_iota(jnp.int32, shape, 0 if transposed else 1)
    return jnp.where((c >= g * factor) & (c < g * factor + factor), 1.0, 0.0).astype(BF)


def row_pack(row, channels):
    blocks = PACK // channels
    part = row.shape[0] // blocks
    return jnp.concatenate([row[k * part : (k + 1) * part] for k in range(blocks)], axis=1)


def row_unpack(packed, channels):
    blocks = PACK // channels
    return jnp.concatenate(
        [packed[:, k * channels : (k + 1) * channels] for k in range(blocks)], axis=0
    )


def col_rows(heights):
    starts, at = [], 0
    for h in heights:
        starts.append(at)
        at += h
    return starts


def channels_last(ref, height, channels):
    eye = group_matrix(channels, channels, 1)
    rows = jnp.swapaxes(ref[...].astype(F32), 0, 1).astype(BF)
    return [dot(rows[r], eye, 0, 0).astype(BF) for r in range(height)]


def pack_edges(n, b, dims, rows, top, bot, left, right):
    heights, widths, channels = dims
    h, w, c = heights[b], widths[b], channels[b]
    start = col_rows(heights)[b]
    for out, row in ((top, rows[0]), (bot, rows[h - 1])):
        out[n, b * 32 : (b + 1) * 32, :] = row_pack(row, c).astype(BF)
        out[n, 128 + b : 129 + b, :c] = row[0:1].astype(BF)
        out[n, 136 + b : 137 + b, :c] = row[w - 1 : w].astype(BF)
    left[n, start : start + h, :c] = stack([row[0:1] for row in rows]).astype(BF)
    right[n, start : start + h, :c] = stack([row[w - 1 : w] for row in rows]).astype(BF)


def gain_row(ref):
    g = ref[...]
    return jnp.concatenate([g[k : k + 1] for k in range(g.shape[0])], axis=1)


def stack(rows):
    return rows[0] if len(rows) == 1 else jnp.concatenate(rows, axis=0)


def upstream_kernel(dims, idx, *refs):
    heights, widths, channels = dims
    d_refs, f_refs, g_refs, x_refs = refs[0:4], refs[4:8], refs[8:12], refs[12:16]
    xt, up_refs, sc_refs = refs[16:20], refs[20:24], refs[24:28]
    inner, outer, left, right, coarse, ends = refs[28:34]
    edges = [ends.at[0], ends.at[1], left, right]
    left[...] = jnp.zeros(left.shape, F32).astype(BF)
    right[...] = jnp.zeros(right.shape, F32).astype(BF)
    ends[:, :, 128:, :] = jnp.zeros((2, 2, 16, PACK), F32).astype(BF)
    dt = []
    for b in range(4):
        if b < 2:
            dt.append(channels_last(d_refs[b], heights[b], channels[b]))
        else:
            dt.append([d_refs[b][r] for r in range(heights[b])])
    mixers = [f_refs[j][...] for j in range(4)]

    def block(j, i):
        off = source_offset(channels, j, i)
        if j == 3:
            return mixers[3][off : off + channels[i]]
        return mixers[j][:, off : off + channels[i]]

    acc = [[dt[i][r].astype(F32) for r in range(heights[i])] for i in range(4)]
    for j in range(4):
        for i in range(j + 1, 4):
            f = 2 ** (i - j)
            pool = group_matrix(widths[i], widths[j], f)
            mat = block(j, i)
            for r in range(heights[i]):
                s = dot(pool, dt[j][r * f])
                for k in range(1, f):
                    s = s + dot(pool, dt[j][r * f + k])
                acc[i][r] = acc[i][r] + dot(s.astype(BF), mat)
        for i in range(j):
            f = 2 ** (j - i)
            spread = group_matrix(widths[j], widths[i], f, True)
            mat = block(j, i)
            for r in range(heights[j]):
                z = dot(spread, dt[j][r]).astype(BF)
                v = dot(z, mat, 1, 1) if j == 3 else dot(z, mat)
                v = v * (1.0 / (f * f))
                for k in range(f):
                    acc[i][r * f + k] = acc[i][r * f + k] + v
    for b in range(4):
        gain = gain_row(g_refs[b])
        scaled = []
        for r in range(heights[b]):
            Packed(up_refs[b], channels[b])[r] = acc[b][r]
            s = (gain * acc[b][r]).astype(BF)
            Packed(sc_refs[b], channels[b])[r] = s
            scaled.append(s.astype(F32))
        flush(up_refs[b], sc_refs[b])
        pack_edges(1, b, dims, scaled, *edges)
        if b < 2:
            rows = channels_last(x_refs[b], heights[b], channels[b])
        else:
            rows = [x_refs[b][r] for r in range(heights[b])]
        for r in range(heights[b]):
            Packed(xt[b], channels[b])[r] = rows[r]
        flush(xt[b])
        pack_edges(0, b, dims, [jnp.maximum(v.astype(F32), 0.0) for v in rows], *edges)
    inner[...] = ends[1 - idx[0]]
    outer[...] = ends[idx[0]]
    w3 = widths[3]
    for r in range(heights[3]):
        coarse[0, r * w3 : (r + 1) * w3] = jnp.maximum(x_refs[3][r].astype(F32), 0.0).astype(BF)
        coarse[1, r * w3 : (r + 1) * w3] = sc_refs[3][r]


class Packed:
    def __init__(self, ref, channels):
        self.ref, self.c, self.two = ref, channels, channels <= 64

    def __getitem__(self, r):
        row = self.ref[r]
        if self.two:
            row = jnp.concatenate([row[:, : self.c], row[:, 64 : 64 + self.c]], axis=0)
        return row

    def __setitem__(self, r, row):
        row = row.astype(F32)
        if self.two:
            half = row.shape[0] // 2
            gap = jnp.zeros((half, 64 - self.c), F32)
            row = jnp.concatenate([row[:half], gap, row[half:], gap], axis=1)
        self.ref[r] = row.astype(BF)


def packed(dims, refs):
    return [Packed(ref, c) for ref, c in zip(refs, dims[2])]


def pick(odd, first, second):
    return jnp.where(odd == 0, first.astype(F32), second.astype(F32))


def fill(scr, n, b, dims, interior, idx, in_row, out_row, in_col, out_col):
    heights, widths, channels = dims
    h, w, c = heights[b], widths[b], channels[b]
    start = col_rows(heights)[b]
    for r in range(h):
        scr[r + 1, LEFT : LEFT + w, :] = interior(r)
    lines = slice(b * 32, (b + 1) * 32)
    core, band = idx[0], idx[1] % 2
    for first, second, at in ((out_row, in_row, 0), (in_row, out_row, h + 1)):
        packed = pick(core, first[n, lines, :], second[n, lines, :])
        scr[at, LEFT : LEFT + w, :] = row_unpack(packed, c)
    for first, second, at in ((out_col, in_col, LEFT - 1), (in_col, out_col, LEFT + w)):
        vals = pick(band, first[n], second[n])
        for r in range(h):
            scr[r + 1, at : at + 1, :] = vals[start + r : start + r + 1, :c]
        scr[0, at : at + 1, :] = vals[16 + b : 17 + b, :c]
        scr[h + 1, at : at + 1, :] = vals[24 + b : 25 + b, :c]


def shifted(scr, h, w, q):
    return [scr[r, LEFT - 1 + q : LEFT - 1 + q + w, :].astype(BF) for r in range(h + 2)]


def side_by_side(scr, h, w, order):
    gap = jnp.zeros((w, 64 - scr.shape[2]), F32)
    rows = []
    for r in range(h + 2):
        parts = []
        for q in order:
            parts += [scr[r, LEFT - 1 + q : LEFT - 1 + q + w, :], gap]
        rows.append(jnp.concatenate(parts, axis=1).astype(BF))
    return rows


def apart(blocks, axis):
    parts = []
    for block in blocks:
        shape = list(block.shape)
        shape[axis] = 64 - shape[axis]
        parts += [block.astype(F32), jnp.zeros(shape, F32)]
    return jnp.concatenate(parts, axis=axis).astype(BF)


def forward_taps(scr, kernel, h, w):
    if scr.shape[2] <= 64:
        rows = side_by_side(scr, h, w, range(3))
        return sum(
            dot(stack(rows[p : p + h]), apart([kernel[p, q] for q in range(3)], 1), 1, 1)
            for p in range(3)
        )
    total = 0
    for q in range(3):
        rows = shifted(scr, h, w, q)
        total = total + sum(dot(stack(rows[p : p + h]), kernel[p, q], 1, 1) for p in range(3))
    return total


def adjoint_taps(scr, kernel, h, w):
    if scr.shape[2] <= 64:
        rows = side_by_side(scr, h, w, (2, 1, 0))
        return sum(
            dot(stack(rows[2 - p : 2 - p + h]), apart([kernel[p, q] for q in range(3)], 0))
            for p in range(3)
        )
    total = 0
    for q in range(3):
        rows = shifted(scr, h, w, 2 - q)
        total = total + sum(dot(stack(rows[2 - p : 2 - p + h]), kernel[p, q]) for p in range(3))
    return total


def weight_grads_kernel(dims, *refs):
    heights, widths, channels = dims
    idx, x_refs, sc_refs = refs[0], packed(dims, refs[1:4]), packed(dims, refs[4:7])
    edges = refs[7:11]
    keep, send, out, *scrs = refs[11:]
    c0, c1, c2 = channels[0], channels[1], channels[2]
    for b in (2, 1, 0):
        h, w, c = heights[b], widths[b], channels[b]
        fill(scrs[b], 0, b, dims, lambda r: jnp.maximum(x_refs[b][r].astype(F32), 0.0), idx, *edges)
        s_all = stack([sc_refs[b][r] for r in range(h)])
        if c <= 64:
            rows = side_by_side(scrs[b], h, w, range(3))
            wide = [dot(s_all, stack(rows[p : p + h]), 0, 0) for p in range(3)]
        for q in range(3):
            if c > 64:
                rows = shifted(scrs[b], h, w, q)
            for p in range(3):
                if c > 64:
                    g = dot(s_all, stack(rows[p : p + h]), 0, 0)
                else:
                    g = wide[p][:, 64 * q : 64 * q + c]
                tap = p * 3 + q
                if b == 2:
                    out[tap * c2 : (tap + 1) * c2, :] = g[:, :128].astype(BF)
                    half = c2 // 2
                    at = 9 * c2 + tap * half
                    both = jnp.concatenate([g[:half, 128:], g[half:, 128:]], axis=1)
                    out[at : at + half, :] = both.astype(BF)
                elif b == 1:
                    at = 9 * c2 * 3 // 2 + tap * c1
                    out[at : at + c1, :c1] = g.astype(BF)
                else:
                    at = 9 * c2 * 3 // 2 + 9 * c1 + (tap // 2) * c0
                    lane = 64 * (tap % 2)
                    out[at : at + c0, lane : lane + c0] = g.astype(BF)
    half = keep.shape[0]
    keep[...] = out[pl.ds(pl.multiple_of(idx[0] * half, 16), half), :]
    send[...] = out[pl.ds(pl.multiple_of((1 - idx[0]) * half, 16), half), :]


def pair_sum_kernel(n_branch, idx, keep, got, coarse, *outs):
    size = outs[0].shape[0]
    for k in range(n_branch):
        at = pl.ds(pl.multiple_of((idx[1] + k) % n_branch * size, 16), size)
        outs[k][...] = (keep[at, :].astype(F32) + got[at, :].astype(F32)).astype(BF)
    outs[-1][...] = coarse[...]


def stack_kernel(count, *refs):
    for k in range(count):
        refs[-1][k] = refs[k][...]


def corner_kernel(idx, left, right, in_row, out_row, inner, outer):
    core, band = idx[0], idx[1] % 2
    cols = []
    for side, at in ((left, 128), (right, 136)):
        in_part, out_part = in_row[:, at : at + 8, :], out_row[:, at : at + 8, :]
        above, below = pick(core, out_part, in_part), pick(core, in_part, out_part)
        cols.append(jnp.concatenate([side[...].astype(F32), above, below], axis=1))
    inner[...] = pick(band, cols[1], cols[0]).astype(BF)
    outer[...] = pick(band, cols[0], cols[1]).astype(BF)


def sum_kernel(count, *refs):
    total = refs[0][...].astype(F32)
    for k in range(1, count):
        total = total + refs[k][...].astype(F32)
    refs[-1][...] = total.astype(BF)


def ordered_sum_kernel(n, idx, *refs):
    held = refs[-1]
    for k in range(n):
        held[(idx[2] + k) % n] = refs[k][...]
    total = held[0].astype(F32)
    for k in range(1, n):
        total = total + held[k].astype(F32)
    refs[n][...] = total.astype(BF)


def forward_kernel(dims, idx, *refs):
    heights, widths, channels = dims
    x_refs = packed(dims, refs[0:4])
    g_refs, f_refs, k_refs = refs[4:8], refs[8:12], refs[12:16]
    edges = refs[16:20]
    refs = refs[20:]
    merged_refs, scrs, wide = refs[0:4], refs[4:8], refs[8:12]
    units = []
    for b in range(4):
        h, w, c = heights[b], widths[b], channels[b]
        fill(scrs[b], 0, b, dims, lambda r: jnp.maximum(x_refs[b][r].astype(F32), 0.0), idx, *edges)
        resp = forward_taps(scrs[b], k_refs[b], h, w)
        gain = gain_row(g_refs[b])
        units.append(
            [
                (x_refs[b][r].astype(F32) + gain * resp[r * w : (r + 1) * w]).astype(BF)
                for r in range(h)
            ]
        )
    mixers = [f_refs[j][...] for j in range(4)]

    def mix(v, j, i):
        off = source_offset(channels, j, i)
        if j == 3:
            return dot(v, mixers[3][off : off + channels[i]])
        return dot(v, mixers[j][:, off : off + channels[i]], 1, 1)

    sums = [[u.astype(F32) for u in units[j]] for j in range(4)]
    for i in range(4):
        for j in range(i + 1, 4):
            f = 2 ** (j - i)
            pool = group_matrix(widths[j], widths[i], f)
            for r in range(heights[j]):
                s = dot(pool, units[i][r * f])
                for k in range(1, f):
                    s = s + dot(pool, units[i][r * f + k])
                s = (s * (1.0 / (f * f))).astype(BF)
                sums[j][r] = sums[j][r] + mix(s, j, i)
        for j in range(i):
            f = 2 ** (i - j)
            spread = group_matrix(widths[i], widths[j], f, True)
            for r in range(heights[i]):
                v = mix(dot(spread, units[i][r]).astype(BF), j, i)
                for k in range(f):
                    sums[j][r * f + k] = sums[j][r * f + k] + v
    for j in range(4):
        emit(j, heights, merged_refs[j], sums[j], wide[j])


def emit(b, heights, out, rows, stage):
    if b >= 2:
        for r in range(heights[b]):
            out[r] = rows[r].astype(BF)
        flush(out)
        return
    for r in range(heights[b]):
        stage[r] = rows[r].T
    out[...] = jnp.swapaxes(stage[...], 0, 1).astype(BF)
    flush(out)


def adjoint_kernel(dims, idx, *refs):
    heights, widths, channels = dims
    x_refs, sc_refs, up_refs = (packed(dims, refs[k : k + 4]) for k in (0, 4, 8))
    k_refs = refs[12:16]
    edges = refs[16:20]
    refs = refs[20:]
    back_refs, scrs, wide = refs[0:4], refs[4:8], refs[8:12]
    for b in range(4):
        h, w, c = heights[b], widths[b], channels[b]
        fill(scrs[b], 1, b, dims, lambda r: sc_refs[b][r].astype(F32), idx, *edges)
        adj = adjoint_taps(scrs[b], k_refs[b], h, w)
        back = [
            up_refs[b][r].astype(F32)
            + jnp.where(x_refs[b][r].astype(F32) > 0, adj[r * w : (r + 1) * w], 0.0)
            for r in range(h)
        ]
        emit(b, heights, back_refs[b], back, wide[b])


def coarse_kernel(dims, n_branch, n_chip, scale, idx, *refs):
    out, act, win, grad, acc, taps, sems = refs[-7:]
    w3, c3 = dims[1][3], dims[2][3]
    rows, cols = 2 * n_chip, n_branch * w3
    act[0] = jnp.zeros(act.shape[1:], F32)
    act[rows + 1] = jnp.zeros(act.shape[1:], F32)
    for r in range(rows):
        act[r + 1, 0:LEFT, :] = jnp.zeros((LEFT, c3), F32)
        act[r + 1, LEFT + cols :, :] = jnp.zeros((8, c3), F32)
    for m in range(2):
        for l in range(n_branch):
            for k in range(n_chip):
                src = refs[m * n_branch + l]
                r = (idx[2] + k) % n_chip * 2 + (idx[0] + m) % 2
                off = pl.multiple_of((idx[1] + l) % n_branch * w3, w3)
                act[r + 1, pl.ds(LEFT + off, w3), :] = src[k, 0].astype(F32)
                win[r, pl.ds(off, w3), :] = src[k, 1]
    for r in range(rows):
        grad[:, r * cols : (r + 1) * cols] = win[r].astype(F32).T.astype(BF)
    span = rows * cols
    step = min(span, 1024)
    copies = []
    for q in range(3):
        for r in range(rows + 2):
            win[r] = act[r, LEFT - 1 + q : LEFT - 1 + q + cols, :].astype(BF)
        for p in range(3):
            if step == span:
                total = dot(grad[...], win[p : p + rows].reshape(span, c3))
            else:
                acc[...] = jnp.zeros(acc.shape, F32)
                lines = step // cols

                @pl.loop(0, rows // lines)
                def _(t, p=p):
                    some = win[pl.ds(t * lines + p, lines)].reshape(step, c3)
                    acc[...] += dot(grad[:, pl.ds(pl.multiple_of(t * step, step), step)], some)

                total = acc[...]
            taps[p, q] = (total * scale).astype(BF)
            copies.append(pltpu.make_async_copy(taps.at[p, q], out.at[p, q], sems.at[p, q]))
            copies[-1].start()
    for copy in copies:
        copy.wait()


def finish_kernel(dims, n_branch, scales, idx, *refs):
    channels = dims[2]
    parts = refs[: 2 * n_branch]
    outs, flat = refs[-4:-1], refs[-1]
    c0, c1, c2 = channels[0], channels[1], channels[2]
    size = parts[0].shape[0]
    for k, part in enumerate(parts):
        core, band = (idx[0] + k // n_branch) % 2, (idx[1] + k) % n_branch
        at = pl.multiple_of((core * n_branch + band) * size, 16)
        flat[pl.ds(at, size), :] = part[...].astype(F32)
    base1 = 9 * c2 * 3 // 2
    base0 = base1 + 9 * c1
    half = c2 // 2
    for tap in range(9):
        p, q = tap // 3, tap % 3
        outs[2][p, q, :, 0:128] = (flat[tap * c2 : (tap + 1) * c2, :] * scales[2]).astype(BF)
        at = 9 * c2 + tap * half
        both = flat[at : at + half, :]
        tail = jnp.concatenate([both[:, :64], both[:, 64:]], axis=0)
        outs[2][p, q, :, 128:c2] = (tail * scales[2]).astype(BF)
        at = base1 + tap * c1
        outs[1][p, q] = (flat[at : at + c1, :c1] * scales[1]).astype(BF)
        at = base0 + (tap // 2) * c0
        lane = 64 * (tap % 2)
        outs[0][p, q] = (flat[at : at + c0, lane : lane + c0] * scales[0]).astype(BF)


def local(*args):
    maps, kernels, gains, mixers, cotans = (args[4 * k : 4 * k + 4] for k in range(5))
    n_rows, n_branch = lax.axis_size("rows"), lax.axis_size("branch")
    n_chip = n_rows // 2
    channels = [a.shape[0] for a in maps]
    heights = [a.shape[1] for a in maps]
    widths = [a.shape[2] for a in maps]
    dims = (heights, widths, channels)
    last = lambda a: jnp.transpose(a, (1, 2, 0))
    unlast = lambda a: jnp.transpose(a, (2, 0, 1))
    xs = [maps[0], maps[1], last(maps[2]), last(maps[3])]
    ds = [cotans[0], cotans[1], last(cotans[2]), last(cotans[3])]
    gs = [g.reshape(-1, 128) if g.shape[0] % 128 == 0 else g.reshape(1, -1) for g in gains]
    fs = [mixers[0], mixers[1], mixers[2], mixers[3].T]
    shapes = [(heights[b], widths[b], channels[b]) for b in range(4)]
    kept = [sds((h, w // 2, 128) if c <= 64 else (h, w, c), BF) for h, w, c in shapes]
    scales = [1.0 / math.sqrt(heights[b] * n_rows * widths[b] * n_branch) for b in range(4)]
    swap = lambda n: [(i, i ^ 1) for i in range(n)]
    hop = lambda n: [(i, i + 1 if i % 2 else i - 1) for i in range(1, n - 1)]
    core_swap = lambda a: lax.ppermute(a, "rows", swap(n_rows))
    from_branch = lambda k: [((i + k) % n_branch, i) for i in range(n_branch)]
    to_branch = lambda k: [(i, (i + k) % n_branch) for i in range(n_branch)]
    from_chip = lambda k: [((i + 2 * k) % n_rows, i) for i in range(n_rows)]

    outs = call(
        functools.partial(upstream_kernel, dims),
        kept * 3 + [sds((2, 144, PACK), BF)] * 2 + [sds((2, 16, PACK), BF)] * 2
        + [sds((2, heights[3] * widths[3], channels[3]), BF)],
        ds + fs + gs + xs,
        [pltpu.VMEM((2, 2, 144, PACK), BF)],
        placed=True, far=range(16), far_out=range(17), limit=WHOLE, flops=6 * 10**9,
    )
    xt, ups, scs = outs[:4], outs[4:8], outs[8:12]
    inner, outer, left, right, coarse = outs[12:]
    out_row = lax.ppermute(outer, "rows", hop(n_rows))
    in_row = core_swap(inner)
    inner, outer = call(
        corner_kernel, [sds((2, 32, PACK), BF)] * 2, [left, right, in_row, out_row],
        placed=True, flops=6 * 10**9,
    )
    out_col = lax.ppermute(outer, "branch", hop(n_branch))
    in_col = lax.ppermute(inner, "branch", swap(n_branch))
    edges = [in_row, out_row, in_col, out_col]

    pad = lambda b: pltpu.VMEM((heights[b] + 2, widths[b] + 16, channels[b]), F32)
    wide = [pltpu.VMEM((heights[b], channels[b], widths[b]), F32) for b in range(4)]
    pieces = 2 * n_branch
    packed_rows = 9 * (channels[2] * 3 // 2 + channels[1]) + 5 * channels[0]
    size = -(-packed_rows // (16 * pieces)) * 16
    part = sds((size, 128), BF)
    keep, send = call(
        functools.partial(weight_grads_kernel, dims),
        [sds((n_branch * size, 128), BF)] * 2,
        list(xt[:3]) + list(scs[:3]) + edges,
        [pltpu.VMEM((pieces * size, 128), BF), pad(0), pad(1), pad(2)],
        placed=True, flops=6 * 10**9,
    )
    *parts, coarse = call(
        functools.partial(pair_sum_kernel, n_branch),
        [part] * n_branch + [sds(coarse.shape, BF)],
        [keep, core_swap(send), coarse],
        placed=True,
    )
    got = [lax.ppermute(parts[k], "branch", to_branch(k)) for k in range(1, n_branch)]
    held = [coarse] + [lax.ppermute(coarse, "rows", from_chip(k)) for k in range(1, n_chip)]
    (part_sum,) = call(
        functools.partial(sum_kernel, n_branch), [part], [parts[0]] + got, deps=held[1:]
    )
    got = [lax.ppermute(part_sum, "rows", from_chip(k)) for k in range(1, n_chip)]
    (held,) = call(
        functools.partial(stack_kernel, n_chip), [sds((n_chip,) + coarse.shape, BF)], held,
        deps=(part_sum,),
    )
    held = [held] + [lax.ppermute(held, "branch", from_branch(k)) for k in range(1, n_branch)]
    *merged, merged_token = call(
        functools.partial(forward_kernel, dims),
        [sds(maps[0].shape, BF), sds(maps[1].shape, BF), sds(shapes[2], BF), sds(shapes[3], BF)],
        list(xt) + gs + fs + list(kernels) + edges,
        [pad(b) for b in range(4)] + wide,
        placed=True, far_out=range(4), token=True, deps=(part_sum,), flops=6 * 10**9,
    )
    *back, back_token = call(
        functools.partial(adjoint_kernel, dims),
        [sds(maps[0].shape, BF), sds(maps[1].shape, BF), sds(shapes[2], BF), sds(shapes[3], BF)],
        list(xt) + list(scs) + list(ups) + list(kernels) + edges,
        [pad(b) for b in range(4)] + wide,
        placed=True, far_out=range(4), token=True, deps=(part_sum,),
    )
    (total,) = call(
        functools.partial(ordered_sum_kernel, n_chip), [part], [part_sum] + got,
        [pltpu.VMEM((n_chip, size, 128), BF)], placed=True, deps=(merged_token, *held[1:]),
    )
    mine = [total] + [lax.ppermute(total, "branch", from_branch(k)) for k in range(1, n_branch)]
    held = held + [core_swap(a) for a in held]
    cols = n_branch * widths[3]
    kgrad3, coarse_token = call(
        functools.partial(coarse_kernel, dims, n_branch, n_chip, scales[3]),
        [sds(kernels[3].shape, BF)],
        held,
        [
            pltpu.VMEM((n_rows + 2, cols + 16, channels[3]), F32),
            pltpu.VMEM((n_rows + 2, cols, channels[3]), BF),
            pltpu.VMEM((channels[3], n_rows * cols), BF),
            pltpu.VMEM((channels[3], channels[3]), F32),
            pltpu.VMEM(kernels[3].shape, BF),
            pltpu.SemaphoreType.DMA((3, 3)),
        ],
        placed=True, raw_out=(0,), token=True, deps=(total,), flops=5 * 10**9, limit=COARSE,
    )
    mine = mine + [core_swap(a) for a in mine]
    kgrads = call(
        functools.partial(finish_kernel, dims, n_branch, scales),
        [sds(k.shape, BF) for k in kernels[:3]],
        mine,
        [pltpu.VMEM((pieces * size, 128), F32)], placed=True, far_out=range(3), deps=(coarse_token, back_token),
    )
    return (
        merged[0], merged[1], unlast(merged[2]), unlast(merged[3]),
        back[0], back[1], unlast(back[2]), unlast(back[3]),
        *kgrads, kgrad3,
    )


def solution(mesh):
    maps = P(None, "rows", "branch")
    in_specs = (maps,) * 4 + (P(),) * 12 + (maps,) * 4
    out_specs = (maps,) * 8 + (P(),) * 4
    return jax.shard_map(
        lambda *args: local(*args),
        mesh=mesh, in_specs=in_specs, out_specs=out_specs, check_vma=False,
    )
```

```python
import functools
import math

import jax
import jax.numpy as jnp
from jax import lax
from jax.experimental import pallas as pl
from jax.experimental.pallas import tpu as pltpu
from jax.sharding import PartitionSpec as P

BF = jnp.bfloat16
F32 = jnp.float32
LEFT = 8
PACK = 384
WHOLE = 61
COARSE = 46
FORWARD, ADJOINT, GATHERED, SMALL = 6 * 10**9, 3 * 10**9, 5 * 10**9, 4 * 10**9


def dot(a, b, ca=1, cb=0):
    return lax.dot_general(a, b, (((ca,), (cb,)), ((), ())), preferred_element_type=F32)


def source_offset(channels, target, source):
    return sum(channels[k] for k in range(source) if k != target)


class Fetched:
    def __init__(self, ref, copy):
        self.ref, self.copy, self.shape = ref, copy, ref.shape
        copy.start()

    def wait(self):
        if self.copy is not None:
            self.copy.wait()
            self.copy = None

    def __getitem__(self, at):
        self.wait()
        return self.ref[at]


class Sent:
    def __init__(self, ref, copy):
        self.ref, self.copy, self.shape, self.started = ref, copy, ref.shape, False

    def __setitem__(self, at, value):
        self.ref[at] = value

    def __getitem__(self, at):
        return self.ref[at]

    def flush(self):
        if not self.started:
            self.copy.start()
            self.started = True

    def wait(self):
        self.flush()
        self.copy.wait()


def flush(*refs):
    for ref in refs:
        if isinstance(ref, Sent):
            ref.flush()


def call(body, outs, args, scratch=(), far=(), far_out=(), placed=False, deps=(), raw_out=(), token=False, flops=SMALL, limit=24):
    far, far_out = list(far), list(far_out)
    if token:
        outs = [*outs, sds((8, 128), F32)]
    n_in, n_out, n_far = len(args), len(outs), len(far)
    n_moved = n_far + len(far_out)

    def wrapped(*refs):
        row = lax.axis_index("rows")
        place = (row % 2, lax.axis_index("branch"), row // 2)
        ins, rest = list(refs[:n_in]), refs[n_in + len(deps) :]
        results, held, sems = list(rest[:n_out]), rest[n_out : n_out + n_moved], rest[-1]
        copy = lambda a, b, k: pltpu.make_async_copy(a, b, sems.at[k])
        for at, k in enumerate(far):
            ins[k] = Fetched(held[at], copy(ins[k], held[at], at))
        for at, k in enumerate(far_out, n_far):
            results[k] = Sent(held[at], copy(held[at], results[k], at))
        if token:
            results.pop()[...] = jnp.zeros((8, 128), F32)
        body(*([place] if placed else []), *ins, *results, *rest[n_out + n_moved : -1])
        for k in far_out:
            results[k].flush()
        for ref in [ins[k] for k in far] + [results[k] for k in far_out]:
            ref.wait()

    def space(k, kept):
        return pl.BlockSpec(memory_space=pl.ANY if k in kept else pltpu.VMEM)

    moved = [args[k] for k in far] + [outs[k] for k in far_out]
    return pl.pallas_call(
        wrapped,
        name=getattr(body, "func", body).__name__,
        out_shape=outs,
        in_specs=[space(k, far) for k in range(n_in)]
        + [pl.BlockSpec(memory_space=pl.ANY) for _ in deps],
        out_specs=[space(k, far_out + list(raw_out)) for k in range(n_out)],
        scratch_shapes=[pltpu.VMEM(a.shape, a.dtype) for a in moved]
        + list(scratch)
        + [pltpu.SemaphoreType.DMA((max(n_moved, 1),))],
        compiler_params=pltpu.CompilerParams(vmem_limit_bytes=limit * 1024 * 1024),
        cost_estimate=pl.CostEstimate(flops=flops, bytes_accessed=10**6, transcendentals=0),
    )(*args, *deps)


def sds(shape, dtype):
    return jax.ShapeDtypeStruct(shape, dtype)


def group_matrix(groups, cells, factor, transposed=False):
    shape = (cells, groups) if transposed else (groups, cells)
    g = lax.broadcasted_iota(jnp.int32, shape, 1 if transposed else 0)
    c = lax.broadcasted_iota(jnp.int32, shape, 0 if transposed else 1)
    return jnp.where((c >= g * factor) & (c < g * factor + factor), 1.0, 0.0).astype(BF)


def row_pack(row, channels):
    blocks = PACK // channels
    part = row.shape[0] // blocks
    return jnp.concatenate([row[k * part : (k + 1) * part] for k in range(blocks)], axis=1)


def row_unpack(packed, channels):
    blocks = PACK // channels
    return jnp.concatenate(
        [packed[:, k * channels : (k + 1) * channels] for k in range(blocks)], axis=0
    )


def col_rows(heights):
    starts, at = [], 0
    for h in heights:
        starts.append(at)
        at += h
    return starts


def channels_last(ref, height, channels):
    eye = group_matrix(channels, channels, 1)
    rows = jnp.swapaxes(ref[...].astype(F32), 0, 1).astype(BF)
    return [dot(rows[r], eye, 0, 0).astype(BF) for r in range(height)]


def pack_edges(n, b, dims, rows, top, bot, left, right):
    heights, widths, channels = dims
    h, w, c = heights[b], widths[b], channels[b]
    start = col_rows(heights)[b]
    for out, row in ((top, rows[0]), (bot, rows[h - 1])):
        out[n, b * 32 : (b + 1) * 32, :] = row_pack(row, c).astype(BF)
        out[n, 128 + b : 129 + b, :c] = row[0:1].astype(BF)
        out[n, 136 + b : 137 + b, :c] = row[w - 1 : w].astype(BF)
    left[n, start : start + h, :c] = stack([row[0:1] for row in rows]).astype(BF)
    right[n, start : start + h, :c] = stack([row[w - 1 : w] for row in rows]).astype(BF)


def gain_row(ref):
    g = ref[...]
    return jnp.concatenate([g[k : k + 1] for k in range(g.shape[0])], axis=1)


def stack(rows):
    return rows[0] if len(rows) == 1 else jnp.concatenate(rows, axis=0)


def upstream_kernel(dims, idx, *refs):
    heights, widths, channels = dims
    d_refs, f_refs, g_refs, x_refs = refs[0:4], refs[4:8], refs[8:12], refs[12:16]
    xt, up_refs, sc_refs = refs[16:20], refs[20:24], refs[24:28]
    inner, outer, left, right, coarse, ends = refs[28:34]
    edges = [ends.at[0], ends.at[1], left, right]
    left[...] = jnp.zeros(left.shape, F32).astype(BF)
    right[...] = jnp.zeros(right.shape, F32).astype(BF)
    ends[:, :, 128:, :] = jnp.zeros((2, 2, 16, PACK), F32).astype(BF)
    dt = []
    for b in range(4):
        if b < 2:
            dt.append(channels_last(d_refs[b], heights[b], channels[b]))
        else:
            dt.append([d_refs[b][r] for r in range(heights[b])])
    mixers = [f_refs[j][...] for j in range(4)]

    def block(j, i):
        off = source_offset(channels, j, i)
        if j == 3:
            return mixers[3][off : off + channels[i]]
        return mixers[j][:, off : off + channels[i]]

    acc = [[dt[i][r].astype(F32) for r in range(heights[i])] for i in range(4)]
    for j in range(4):
        for i in range(j + 1, 4):
            f = 2 ** (i - j)
            pool = group_matrix(widths[i], widths[j], f)
            mat = block(j, i)
            for r in range(heights[i]):
                s = dot(pool, dt[j][r * f])
                for k in range(1, f):
                    s = s + dot(pool, dt[j][r * f + k])
                acc[i][r] = acc[i][r] + dot(s.astype(BF), mat)
        for i in range(j):
            f = 2 ** (j - i)
            spread = group_matrix(widths[j], widths[i], f, True)
            mat = block(j, i)
            for r in range(heights[j]):
                z = dot(spread, dt[j][r]).astype(BF)
                v = dot(z, mat, 1, 1) if j == 3 else dot(z, mat)
                v = v * (1.0 / (f * f))
                for k in range(f):
                    acc[i][r * f + k] = acc[i][r * f + k] + v
    for b in range(4):
        gain = gain_row(g_refs[b])
        scaled = []
        for r in range(heights[b]):
            Packed(up_refs[b], channels[b])[r] = acc[b][r]
            s = (gain * acc[b][r]).astype(BF)
            Packed(sc_refs[b], channels[b])[r] = s
            scaled.append(s.astype(F32))
        flush(up_refs[b], sc_refs[b])
        pack_edges(1, b, dims, scaled, *edges)
        if b < 2:
            rows = channels_last(x_refs[b], heights[b], channels[b])
        else:
            rows = [x_refs[b][r] for r in range(heights[b])]
        for r in range(heights[b]):
            Packed(xt[b], channels[b])[r] = rows[r]
        flush(xt[b])
        pack_edges(0, b, dims, [jnp.maximum(v.astype(F32), 0.0) for v in rows], *edges)
    inner[...] = ends[1 - idx[0]]
    outer[...] = ends[idx[0]]
    w3 = widths[3]
    for r in range(heights[3]):
        coarse[0, r * w3 : (r + 1) * w3] = jnp.maximum(x_refs[3][r].astype(F32), 0.0).astype(BF)
        coarse[1, r * w3 : (r + 1) * w3] = sc_refs[3][r]


class Packed:
    def __init__(self, ref, channels):
        self.ref, self.c, self.two = ref, channels, channels <= 64

    def __getitem__(self, r):
        row = self.ref[r]
        if self.two:
            row = jnp.concatenate([row[:, : self.c], row[:, 64 : 64 + self.c]], axis=0)
        return row

    def __setitem__(self, r, row):
        row = row.astype(F32)
        if self.two:
            half = row.shape[0] // 2
            gap = jnp.zeros((half, 64 - self.c), F32)
            row = jnp.concatenate([row[:half], gap, row[half:], gap], axis=1)
        self.ref[r] = row.astype(BF)


def packed(dims, refs):
    return [Packed(ref, c) for ref, c in zip(refs, dims[2])]


def pick(odd, first, second):
    return jnp.where(odd == 0, first.astype(F32), second.astype(F32))


def fill(scr, n, b, dims, interior, idx, in_row, out_row, in_col, out_col):
    heights, widths, channels = dims
    h, w, c = heights[b], widths[b], channels[b]
    start = col_rows(heights)[b]
    for r in range(h):
        scr[r + 1, LEFT : LEFT + w, :] = interior(r)
    lines = slice(b * 32, (b + 1) * 32)
    core, band = idx[0], idx[1] % 2
    for first, second, at in ((out_row, in_row, 0), (in_row, out_row, h + 1)):
        packed = pick(core, first[n, lines, :], second[n, lines, :])
        scr[at, LEFT : LEFT + w, :] = row_unpack(packed, c)
    for first, second, at in ((out_col, in_col, LEFT - 1), (in_col, out_col, LEFT + w)):
        vals = pick(band, first[n], second[n])
        for r in range(h):
            scr[r + 1, at : at + 1, :] = vals[start + r : start + r + 1, :c]
        scr[0, at : at + 1, :] = vals[16 + b : 17 + b, :c]
        scr[h + 1, at : at + 1, :] = vals[24 + b : 25 + b, :c]


def shifted(scr, h, w, q):
    return [scr[r, LEFT - 1 + q : LEFT - 1 + q + w, :].astype(BF) for r in range(h + 2)]


def side_by_side(scr, h, w, order):
    gap = jnp.zeros((w, 64 - scr.shape[2]), F32)
    rows = []
    for r in range(h + 2):
        parts = []
        for q in order:
            parts += [scr[r, LEFT - 1 + q : LEFT - 1 + q + w, :], gap]
        rows.append(jnp.concatenate(parts, axis=1).astype(BF))
    return rows


def apart(blocks, axis):
    parts = []
    for block in blocks:
        shape = list(block.shape)
        shape[axis] = 64 - shape[axis]
        parts += [block.astype(F32), jnp.zeros(shape, F32)]
    return jnp.concatenate(parts, axis=axis).astype(BF)


def forward_taps(scr, kernel, h, w):
    if scr.shape[2] <= 64:
        rows = side_by_side(scr, h, w, range(3))
        return sum(
            dot(stack(rows[p : p + h]), apart([kernel[p, q] for q in range(3)], 1), 1, 1)
            for p in range(3)
        )
    total = 0
    for q in range(3):
        rows = shifted(scr, h, w, q)
        total = total + sum(dot(stack(rows[p : p + h]), kernel[p, q], 1, 1) for p in range(3))
    return total


def adjoint_taps(scr, kernel, h, w):
    if scr.shape[2] <= 64:
        rows = side_by_side(scr, h, w, (2, 1, 0))
        return sum(
            dot(stack(rows[2 - p : 2 - p + h]), apart([kernel[p, q] for q in range(3)], 0))
            for p in range(3)
        )
    total = 0
    for q in range(3):
        rows = shifted(scr, h, w, 2 - q)
        total = total + sum(dot(stack(rows[2 - p : 2 - p + h]), kernel[p, q]) for p in range(3))
    return total


def weight_grads_kernel(dims, *refs):
    heights, widths, channels = dims
    idx, x_refs, sc_refs = refs[0], packed(dims, refs[1:4]), packed(dims, refs[4:7])
    edges = refs[7:11]
    keep, send, out, *scrs = refs[11:]
    c0, c1, c2 = channels[0], channels[1], channels[2]
    for b in (2, 1, 0):
        h, w, c = heights[b], widths[b], channels[b]
        fill(scrs[b], 0, b, dims, lambda r: jnp.maximum(x_refs[b][r].astype(F32), 0.0), idx, *edges)
        s_all = stack([sc_refs[b][r] for r in range(h)])
        if c <= 64:
            rows = side_by_side(scrs[b], h, w, range(3))
            wide = [dot(s_all, stack(rows[p : p + h]), 0, 0) for p in range(3)]
        for q in range(3):
            if c > 64:
                rows = shifted(scrs[b], h, w, q)
            for p in range(3):
                if c > 64:
                    g = dot(s_all, stack(rows[p : p + h]), 0, 0)
                else:
                    g = wide[p][:, 64 * q : 64 * q + c]
                tap = p * 3 + q
                if b == 2:
                    out[tap * c2 : (tap + 1) * c2, :] = g[:, :128].astype(BF)
                    half = c2 // 2
                    at = 9 * c2 + tap * half
                    both = jnp.concatenate([g[:half, 128:], g[half:, 128:]], axis=1)
                    out[at : at + half, :] = both.astype(BF)
                elif b == 1:
                    at = 9 * c2 * 3 // 2 + tap * c1
                    out[at : at + c1, :c1] = g.astype(BF)
                else:
                    at = 9 * c2 * 3 // 2 + 9 * c1 + (tap // 2) * c0
                    lane = 64 * (tap % 2)
                    out[at : at + c0, lane : lane + c0] = g.astype(BF)
    half = keep.shape[0]
    keep[...] = out[pl.ds(pl.multiple_of(idx[0] * half, 16), half), :]
    send[...] = out[pl.ds(pl.multiple_of((1 - idx[0]) * half, 16), half), :]


def pair_sum_kernel(n_branch, idx, keep, got, coarse, *outs):
    size = outs[0].shape[0]
    for k in range(n_branch):
        at = pl.ds(pl.multiple_of((idx[1] + k) % n_branch * size, 16), size)
        outs[k][...] = (keep[at, :].astype(F32) + got[at, :].astype(F32)).astype(BF)
    outs[-1][...] = coarse[...]


def stack_kernel(count, *refs):
    for k in range(count):
        refs[-1][k] = refs[k][...]


def corner_kernel(idx, left, right, in_row, out_row, inner, outer):
    core, band = idx[0], idx[1] % 2
    cols = []
    for side, at in ((left, 128), (right, 136)):
        in_part, out_part = in_row[:, at : at + 8, :], out_row[:, at : at + 8, :]
        above, below = pick(core, out_part, in_part), pick(core, in_part, out_part)
        cols.append(jnp.concatenate([side[...].astype(F32), above, below], axis=1))
    inner[...] = pick(band, cols[1], cols[0]).astype(BF)
    outer[...] = pick(band, cols[0], cols[1]).astype(BF)


def sum_kernel(count, *refs):
    total = refs[0][...].astype(F32)
    for k in range(1, count):
        total = total + refs[k][...].astype(F32)
    refs[-1][...] = total.astype(BF)


def ordered_sum_kernel(n, idx, *refs):
    held = refs[-1]
    for k in range(n):
        held[(idx[2] + k) % n] = refs[k][...]
    total = held[0].astype(F32)
    for k in range(1, n):
        total = total + held[k].astype(F32)
    refs[n][...] = total.astype(BF)


def forward_kernel(dims, idx, *refs):
    heights, widths, channels = dims
    x_refs = packed(dims, refs[0:4])
    g_refs, f_refs, k_refs = refs[4:8], refs[8:12], refs[12:16]
    edges = refs[16:20]
    refs = refs[20:]
    merged_refs, scrs, wide = refs[0:4], refs[4:8], refs[8:12]
    units = []
    for b in range(4):
        h, w, c = heights[b], widths[b], channels[b]
        fill(scrs[b], 0, b, dims, lambda r: jnp.maximum(x_refs[b][r].astype(F32), 0.0), idx, *edges)
        resp = forward_taps(scrs[b], k_refs[b], h, w)
        gain = gain_row(g_refs[b])
        units.append(
            [
                (x_refs[b][r].astype(F32) + gain * resp[r * w : (r + 1) * w]).astype(BF)
                for r in range(h)
            ]
        )
    mixers = [f_refs[j][...] for j in range(4)]

    def mix(v, j, i):
        off = source_offset(channels, j, i)
        if j == 3:
            return dot(v, mixers[3][off : off + channels[i]])
        return dot(v, mixers[j][:, off : off + channels[i]], 1, 1)

    sums = [[u.astype(F32) for u in units[j]] for j in range(4)]
    for i in range(4):
        for j in range(i + 1, 4):
            f = 2 ** (j - i)
            pool = group_matrix(widths[j], widths[i], f)
            for r in range(heights[j]):
                s = dot(pool, units[i][r * f])
                for k in range(1, f):
                    s = s + dot(pool, units[i][r * f + k])
                s = (s * (1.0 / (f * f))).astype(BF)
                sums[j][r] = sums[j][r] + mix(s, j, i)
        for j in range(i):
            f = 2 ** (i - j)
            spread = group_matrix(widths[i], widths[j], f, True)
            for r in range(heights[i]):
                v = mix(dot(spread, units[i][r]).astype(BF), j, i)
                for k in range(f):
                    sums[j][r * f + k] = sums[j][r * f + k] + v
    for j in range(4):
        emit(j, heights, merged_refs[j], sums[j], wide[j])


def emit(b, heights, out, rows, stage):
    if b >= 2:
        for r in range(heights[b]):
            out[r] = rows[r].astype(BF)
        flush(out)
        return
    for r in range(heights[b]):
        stage[r] = rows[r].T
    out[...] = jnp.swapaxes(stage[...], 0, 1).astype(BF)
    flush(out)


def adjoint_kernel(dims, idx, *refs):
    heights, widths, channels = dims
    x_refs, sc_refs, up_refs = (packed(dims, refs[k : k + 4]) for k in (0, 4, 8))
    k_refs = refs[12:16]
    edges = refs[16:20]
    refs = refs[20:]
    back_refs, scrs, wide = refs[0:4], refs[4:8], refs[8:12]
    for b in range(4):
        h, w, c = heights[b], widths[b], channels[b]
        fill(scrs[b], 1, b, dims, lambda r: sc_refs[b][r].astype(F32), idx, *edges)
        adj = adjoint_taps(scrs[b], k_refs[b], h, w)
        back = [
            up_refs[b][r].astype(F32)
            + jnp.where(x_refs[b][r].astype(F32) > 0, adj[r * w : (r + 1) * w], 0.0)
            for r in range(h)
        ]
        emit(b, heights, back_refs[b], back, wide[b])


def coarse_kernel(dims, n_branch, n_chip, scale, idx, *refs):
    out, act, win, grad, acc, taps, sems = refs[-7:]
    w3, c3 = dims[1][3], dims[2][3]
    rows, cols = 2 * n_chip, n_branch * w3
    act[0] = jnp.zeros(act.shape[1:], F32)
    act[rows + 1] = jnp.zeros(act.shape[1:], F32)
    for r in range(rows):
        act[r + 1, 0:LEFT, :] = jnp.zeros((LEFT, c3), F32)
        act[r + 1, LEFT + cols :, :] = jnp.zeros((8, c3), F32)
    for m in range(2):
        for l in range(n_branch):
            for k in range(n_chip):
                src = refs[m * n_branch + l]
                r = (idx[2] + k) % n_chip * 2 + (idx[0] + m) % 2
                off = pl.multiple_of((idx[1] + l) % n_branch * w3, w3)
                act[r + 1, pl.ds(LEFT + off, w3), :] = src[k, 0].astype(F32)
                win[r, pl.ds(off, w3), :] = src[k, 1]
    for r in range(rows):
        grad[:, r * cols : (r + 1) * cols] = win[r].astype(F32).T.astype(BF)
    span = rows * cols
    step = min(span, 1024)
    copies = []
    for q in range(3):
        for r in range(rows + 2):
            win[r] = act[r, LEFT - 1 + q : LEFT - 1 + q + cols, :].astype(BF)
        for p in range(3):
            if step == span:
                total = dot(grad[...], win[p : p + rows].reshape(span, c3))
            else:
                acc[...] = jnp.zeros(acc.shape, F32)
                lines = step // cols

                @pl.loop(0, rows // lines)
                def _(t, p=p):
                    some = win[pl.ds(t * lines + p, lines)].reshape(step, c3)
                    acc[...] += dot(grad[:, pl.ds(pl.multiple_of(t * step, step), step)], some)

                total = acc[...]
            taps[p, q] = (total * scale).astype(BF)
            copies.append(pltpu.make_async_copy(taps.at[p, q], out.at[p, q], sems.at[p, q]))
            copies[-1].start()
    for copy in copies:
        copy.wait()


def finish_kernel(dims, n_branch, scales, idx, *refs):
    channels = dims[2]
    own, other, *outs, flat = refs
    c0, c1, c2 = channels[0], channels[1], channels[2]
    size = own.shape[1]
    for k in range(n_branch):
        for part, core in ((own, idx[0]), (other, 1 - idx[0])):
            at = pl.multiple_of((core * n_branch + (idx[1] + k) % n_branch) * size, 16)
            flat[pl.ds(at, size), :] = part[k].astype(F32)
    base1 = 9 * c2 * 3 // 2
    base0 = base1 + 9 * c1
    half = c2 // 2
    for tap in range(9):
        p, q = tap // 3, tap % 3
        outs[2][p, q, :, 0:128] = (flat[tap * c2 : (tap + 1) * c2, :] * scales[2]).astype(BF)
        at = 9 * c2 + tap * half
        both = flat[at : at + half, :]
        tail = jnp.concatenate([both[:, :64], both[:, 64:]], axis=0)
        outs[2][p, q, :, 128:c2] = (tail * scales[2]).astype(BF)
        at = base1 + tap * c1
        outs[1][p, q] = (flat[at : at + c1, :c1] * scales[1]).astype(BF)
        at = base0 + (tap // 2) * c0
        lane = 64 * (tap % 2)
        outs[0][p, q] = (flat[at : at + c0, lane : lane + c0] * scales[0]).astype(BF)


def local(*args):
    maps, kernels, gains, mixers, cotans = (args[4 * k : 4 * k + 4] for k in range(5))
    n_rows, n_branch = lax.axis_size("rows"), lax.axis_size("branch")
    n_chip = n_rows // 2
    channels = [a.shape[0] for a in maps]
    heights = [a.shape[1] for a in maps]
    widths = [a.shape[2] for a in maps]
    dims = (heights, widths, channels)
    last = lambda a: jnp.transpose(a, (1, 2, 0))
    unlast = lambda a: jnp.transpose(a, (2, 0, 1))
    xs = [maps[0], maps[1], last(maps[2]), last(maps[3])]
    ds = [cotans[0], cotans[1], last(cotans[2]), last(cotans[3])]
    gs = [g.reshape(-1, 128) if g.shape[0] % 128 == 0 else g.reshape(1, -1) for g in gains]
    fs = [mixers[0], mixers[1], mixers[2], mixers[3].T]
    shapes = [(heights[b], widths[b], channels[b]) for b in range(4)]
    kept = [sds((h, w // 2, 128) if c <= 64 else (h, w, c), BF) for h, w, c in shapes]
    scales = [1.0 / math.sqrt(heights[b] * n_rows * widths[b] * n_branch) for b in range(4)]
    swap = lambda n: [(i, i ^ 1) for i in range(n)]
    hop = lambda n: [(i, i + 1 if i % 2 else i - 1) for i in range(1, n - 1)]
    core_swap = lambda a: lax.ppermute(a, "rows", swap(n_rows))
    from_branch = lambda k: [((i + k) % n_branch, i) for i in range(n_branch)]
    to_branch = lambda k: [(i, (i + k) % n_branch) for i in range(n_branch)]
    from_chip = lambda k: [((i + 2 * k) % n_rows, i) for i in range(n_rows)]

    outs = call(
        functools.partial(upstream_kernel, dims),
        kept * 3 + [sds((2, 144, PACK), BF)] * 2 + [sds((2, 16, PACK), BF)] * 2
        + [sds((2, heights[3] * widths[3], channels[3]), BF)],
        ds + fs + gs + xs,
        [pltpu.VMEM((2, 2, 144, PACK), BF)],
        placed=True, far=range(16), far_out=range(17), limit=WHOLE, flops=6 * 10**9,
    )
    xt, ups, scs = outs[:4], outs[4:8], outs[8:12]
    inner, outer, left, right, coarse = outs[12:]
    out_row = lax.ppermute(outer, "rows", hop(n_rows))
    in_row = core_swap(inner)
    inner, outer = call(
        corner_kernel, [sds((2, 32, PACK), BF)] * 2, [left, right, in_row, out_row],
        placed=True, flops=6 * 10**9,
    )
    out_col = lax.ppermute(outer, "branch", hop(n_branch))
    in_col = lax.ppermute(inner, "branch", swap(n_branch))
    edges = [in_row, out_row, in_col, out_col]

    pad = lambda b: pltpu.VMEM((heights[b] + 2, widths[b] + 16, channels[b]), F32)
    wide = [pltpu.VMEM((heights[b], channels[b], widths[b]), F32) for b in range(4)]
    pieces = 2 * n_branch
    packed_rows = 9 * (channels[2] * 3 // 2 + channels[1]) + 5 * channels[0]
    size = -(-packed_rows // (16 * pieces)) * 16
    part = sds((size, 128), BF)
    keep, send = call(
        functools.partial(weight_grads_kernel, dims),
        [sds((n_branch * size, 128), BF)] * 2,
        list(xt[:3]) + list(scs[:3]) + edges,
        [pltpu.VMEM((pieces * size, 128), BF), pad(0), pad(1), pad(2)],
        placed=True, flops=6 * 10**9,
    )
    *parts, coarse = call(
        functools.partial(pair_sum_kernel, n_branch),
        [part] * n_branch + [sds(coarse.shape, BF)],
        [keep, core_swap(send), coarse],
        placed=True,
    )
    got = [lax.ppermute(parts[k], "branch", to_branch(k)) for k in range(1, n_branch)]
    held = [coarse] + [lax.ppermute(coarse, "rows", from_chip(k)) for k in range(1, n_chip)]
    *back, back_token = call(
        functools.partial(adjoint_kernel, dims),
        [sds(maps[0].shape, BF), sds(maps[1].shape, BF), sds(shapes[2], BF), sds(shapes[3], BF)],
        list(xt) + list(scs) + list(ups) + list(kernels) + edges,
        [pad(b) for b in range(4)] + wide,
        placed=True, far_out=range(4), token=True, deps=(parts[0],), flops=ADJOINT,
    )
    (part_sum,) = call(
        functools.partial(sum_kernel, n_branch), [part], [parts[0]] + got, deps=(back_token, *held[1:])
    )
    got = [lax.ppermute(part_sum, "rows", from_chip(k)) for k in range(1, n_chip)]
    (held,) = call(
        functools.partial(stack_kernel, n_chip), [sds((n_chip,) + coarse.shape, BF)], held,
        deps=(part_sum,),
    )
    held = [held] + [lax.ppermute(held, "branch", from_branch(k)) for k in range(1, n_branch)]
    *merged, merged_token = call(
        functools.partial(forward_kernel, dims),
        [sds(maps[0].shape, BF), sds(maps[1].shape, BF), sds(shapes[2], BF), sds(shapes[3], BF)],
        list(xt) + gs + fs + list(kernels) + edges,
        [pad(b) for b in range(4)] + wide,
        placed=True, far_out=range(4), token=True, deps=(part_sum,), flops=FORWARD,
    )
    (total,) = call(
        functools.partial(ordered_sum_kernel, n_chip), [part], [part_sum] + got,
        [pltpu.VMEM((n_chip, size, 128), BF)], placed=True, deps=(merged_token, *held[1:]),
    )
    mine = [total] + [lax.ppermute(total, "branch", from_branch(k)) for k in range(1, n_branch)]
    held = held + [core_swap(a) for a in held]
    cols = n_branch * widths[3]
    kgrad3, coarse_token = call(
        functools.partial(coarse_kernel, dims, n_branch, n_chip, scales[3]),
        [sds(kernels[3].shape, BF)],
        held,
        [
            pltpu.VMEM((n_rows + 2, cols + 16, channels[3]), F32),
            pltpu.VMEM((n_rows + 2, cols, channels[3]), BF),
            pltpu.VMEM((channels[3], n_rows * cols), BF),
            pltpu.VMEM((channels[3], channels[3]), F32),
            pltpu.VMEM(kernels[3].shape, BF),
            pltpu.SemaphoreType.DMA((3, 3)),
        ],
        placed=True, raw_out=(0,), token=True, deps=(total,), flops=GATHERED, limit=COARSE,
    )
    (mine,) = call(
        functools.partial(stack_kernel, n_branch), [sds((n_branch, size, 128), BF)], mine,
        deps=(coarse_token, back_token,),
    )
    kgrads = call(
        functools.partial(finish_kernel, dims, n_branch, scales),
        [sds(k.shape, BF) for k in kernels[:3]],
        [mine, core_swap(mine)],
        [pltpu.VMEM((pieces * size, 128), F32)], placed=True, far_out=range(3),
    )
    return (
        merged[0], merged[1], unlast(merged[2]), unlast(merged[3]),
        back[0], back[1], unlast(back[2]), unlast(back[3]),
        *kgrads, kgrad3,
    )


def solution(mesh):
    maps = P(None, "rows", "branch")
    in_specs = (maps,) * 4 + (P(),) * 12 + (maps,) * 4
    out_specs = (maps,) * 8 + (P(),) * 4
    return jax.shard_map(
        lambda *args: local(*args),
        mesh=mesh, in_specs=in_specs, out_specs=out_specs, check_vma=False,
    )
```

```python
import functools
import math

import jax
import jax.numpy as jnp
from jax import lax
from jax.experimental import pallas as pl
from jax.experimental.pallas import tpu as pltpu
from jax.sharding import PartitionSpec as P

BF = jnp.bfloat16
F32 = jnp.float32
LEFT = 8
PACK = 384
WHOLE = 61
COARSE = 46
FORWARD, ADJOINT, GATHERED, SMALL = 6 * 10**9, 3 * 10**9, 5 * 10**9, 4 * 10**9


def dot(a, b, ca=1, cb=0):
    return lax.dot_general(a, b, (((ca,), (cb,)), ((), ())), preferred_element_type=F32)


def source_offset(channels, target, source):
    return sum(channels[k] for k in range(source) if k != target)


class Fetched:
    def __init__(self, ref, copy):
        self.ref, self.copy, self.shape = ref, copy, ref.shape
        copy.start()

    def wait(self):
        if self.copy is not None:
            self.copy.wait()
            self.copy = None

    def __getitem__(self, at):
        self.wait()
        return self.ref[at]


class Sent:
    def __init__(self, ref, copy):
        self.ref, self.copy, self.shape, self.started = ref, copy, ref.shape, False

    def __setitem__(self, at, value):
        self.ref[at] = value

    def __getitem__(self, at):
        return self.ref[at]

    def flush(self):
        if not self.started:
            self.copy.start()
            self.started = True

    def wait(self):
        self.flush()
        self.copy.wait()


def flush(*refs):
    for ref in refs:
        if isinstance(ref, Sent):
            ref.flush()


def call(body, outs, args, scratch=(), far=(), far_out=(), placed=False, deps=(), raw_out=(), token=False, flops=SMALL, limit=24):
    far, far_out = list(far), list(far_out)
    if token:
        outs = [*outs, sds((8, 128), F32)]
    n_in, n_out, n_far = len(args), len(outs), len(far)
    n_moved = n_far + len(far_out)

    def wrapped(*refs):
        row = lax.axis_index("rows")
        place = (row % 2, lax.axis_index("branch"), row // 2)
        ins, rest = list(refs[:n_in]), refs[n_in + len(deps) :]
        results, held, sems = list(rest[:n_out]), rest[n_out : n_out + n_moved], rest[-1]
        copy = lambda a, b, k: pltpu.make_async_copy(a, b, sems.at[k])
        for at, k in enumerate(far):
            ins[k] = Fetched(held[at], copy(ins[k], held[at], at))
        for at, k in enumerate(far_out, n_far):
            results[k] = Sent(held[at], copy(held[at], results[k], at))
        if token:
            results.pop()[...] = jnp.zeros((8, 128), F32)
        body(*([place] if placed else []), *ins, *results, *rest[n_out + n_moved : -1])
        for k in far_out:
            results[k].flush()
        for ref in [ins[k] for k in far] + [results[k] for k in far_out]:
            ref.wait()

    def space(k, kept):
        return pl.BlockSpec(memory_space=pl.ANY if k in kept else pltpu.VMEM)

    moved = [args[k] for k in far] + [outs[k] for k in far_out]
    return pl.pallas_call(
        wrapped,
        name=getattr(body, "func", body).__name__,
        out_shape=outs,
        in_specs=[space(k, far) for k in range(n_in)]
        + [pl.BlockSpec(memory_space=pl.ANY) for _ in deps],
        out_specs=[space(k, far_out + list(raw_out)) for k in range(n_out)],
        scratch_shapes=[pltpu.VMEM(a.shape, a.dtype) for a in moved]
        + list(scratch)
        + [pltpu.SemaphoreType.DMA((max(n_moved, 1),))],
        compiler_params=pltpu.CompilerParams(vmem_limit_bytes=limit * 1024 * 1024),
        cost_estimate=pl.CostEstimate(flops=flops, bytes_accessed=10**6, transcendentals=0),
    )(*args, *deps)


def sds(shape, dtype):
    return jax.ShapeDtypeStruct(shape, dtype)


def group_matrix(groups, cells, factor, transposed=False):
    shape = (cells, groups) if transposed else (groups, cells)
    g = lax.broadcasted_iota(jnp.int32, shape, 1 if transposed else 0)
    c = lax.broadcasted_iota(jnp.int32, shape, 0 if transposed else 1)
    return jnp.where((c >= g * factor) & (c < g * factor + factor), 1.0, 0.0).astype(BF)


def row_pack(row, channels):
    blocks = PACK // channels
    part = row.shape[0] // blocks
    return jnp.concatenate([row[k * part : (k + 1) * part] for k in range(blocks)], axis=1)


def row_unpack(packed, channels):
    blocks = PACK // channels
    return jnp.concatenate(
        [packed[:, k * channels : (k + 1) * channels] for k in range(blocks)], axis=0
    )


def col_rows(heights):
    starts, at = [], 0
    for h in heights:
        starts.append(at)
        at += h
    return starts


def channels_last(ref, height, channels):
    eye = group_matrix(channels, channels, 1)
    rows = jnp.swapaxes(ref[...].astype(F32), 0, 1).astype(BF)
    return [dot(rows[r], eye, 0, 0).astype(BF) for r in range(height)]


def pack_edges(n, b, dims, rows, top, bot, left, right):
    heights, widths, channels = dims
    h, w, c = heights[b], widths[b], channels[b]
    start = col_rows(heights)[b]
    for out, row in ((top, rows[0]), (bot, rows[h - 1])):
        out[n, b * 32 : (b + 1) * 32, :] = row_pack(row, c).astype(BF)
        out[n, 128 + b : 129 + b, :c] = row[0:1].astype(BF)
        out[n, 136 + b : 137 + b, :c] = row[w - 1 : w].astype(BF)
    left[n, start : start + h, :c] = stack([row[0:1] for row in rows]).astype(BF)
    right[n, start : start + h, :c] = stack([row[w - 1 : w] for row in rows]).astype(BF)


def gain_row(ref):
    g = ref[...]
    return jnp.concatenate([g[k : k + 1] for k in range(g.shape[0])], axis=1)


def stack(rows):
    return rows[0] if len(rows) == 1 else jnp.concatenate(rows, axis=0)


def upstream_kernel(dims, idx, *refs):
    heights, widths, channels = dims
    d_refs, f_refs, g_refs, x_refs = refs[0:4], refs[4:8], refs[8:12], refs[12:16]
    xt, up_refs, sc_refs = refs[16:20], refs[20:24], refs[24:28]
    inner, outer, sides, coarse, ends = refs[28:33]
    edges = [ends.at[0], ends.at[1], sides.ref.at[0], sides.ref.at[1]]
    sides[...] = jnp.zeros(sides.shape, F32).astype(BF)
    ends[:, :, 128:, :] = jnp.zeros((2, 2, 16, PACK), F32).astype(BF)
    dt = []
    for b in range(4):
        if b < 2:
            dt.append(channels_last(d_refs[b], heights[b], channels[b]))
        else:
            dt.append([d_refs[b][r] for r in range(heights[b])])
    mixers = [f_refs[j][...] for j in range(4)]

    def block(j, i):
        off = source_offset(channels, j, i)
        if j == 3:
            return mixers[3][off : off + channels[i]]
        return mixers[j][:, off : off + channels[i]]

    acc = [[dt[i][r].astype(F32) for r in range(heights[i])] for i in range(4)]
    for j in range(4):
        for i in range(j + 1, 4):
            f = 2 ** (i - j)
            pool = group_matrix(widths[i], widths[j], f)
            mat = block(j, i)
            for r in range(heights[i]):
                s = dot(pool, dt[j][r * f])
                for k in range(1, f):
                    s = s + dot(pool, dt[j][r * f + k])
                acc[i][r] = acc[i][r] + dot(s.astype(BF), mat)
        for i in range(j):
            f = 2 ** (j - i)
            spread = group_matrix(widths[j], widths[i], f, True)
            mat = block(j, i)
            for r in range(heights[j]):
                z = dot(spread, dt[j][r]).astype(BF)
                v = dot(z, mat, 1, 1) if j == 3 else dot(z, mat)
                v = v * (1.0 / (f * f))
                for k in range(f):
                    acc[i][r * f + k] = acc[i][r * f + k] + v
    for b in range(4):
        gain = gain_row(g_refs[b])
        scaled = []
        for r in range(heights[b]):
            Packed(up_refs[b], channels[b])[r] = acc[b][r]
            s = (gain * acc[b][r]).astype(BF)
            Packed(sc_refs[b], channels[b])[r] = s
            scaled.append(s.astype(F32))
        flush(up_refs[b], sc_refs[b])
        pack_edges(1, b, dims, scaled, *edges)
        if b < 2:
            rows = channels_last(x_refs[b], heights[b], channels[b])
        else:
            rows = [x_refs[b][r] for r in range(heights[b])]
        for r in range(heights[b]):
            Packed(xt[b], channels[b])[r] = rows[r]
        flush(xt[b])
        pack_edges(0, b, dims, [jnp.maximum(v.astype(F32), 0.0) for v in rows], *edges)
    inner[...] = ends[1 - idx[0]]
    outer[...] = ends[idx[0]]
    w3 = widths[3]
    for r in range(heights[3]):
        coarse[0, r * w3 : (r + 1) * w3] = jnp.maximum(x_refs[3][r].astype(F32), 0.0).astype(BF)
        coarse[1, r * w3 : (r + 1) * w3] = sc_refs[3][r]


class Packed:
    def __init__(self, ref, channels):
        self.ref, self.c, self.two = ref, channels, channels <= 64

    def __getitem__(self, r):
        row = self.ref[r]
        if self.two:
            row = jnp.concatenate([row[:, : self.c], row[:, 64 : 64 + self.c]], axis=0)
        return row

    def __setitem__(self, r, row):
        row = row.astype(F32)
        if self.two:
            half = row.shape[0] // 2
            gap = jnp.zeros((half, 64 - self.c), F32)
            row = jnp.concatenate([row[:half], gap, row[half:], gap], axis=1)
        self.ref[r] = row.astype(BF)


def packed(dims, refs):
    return [Packed(ref, c) for ref, c in zip(refs, dims[2])]


def pick(odd, first, second):
    return jnp.where(odd == 0, first.astype(F32), second.astype(F32))


def fill(scr, n, b, dims, interior, idx, in_row, out_row, in_col, out_col):
    heights, widths, channels = dims
    h, w, c = heights[b], widths[b], channels[b]
    start = col_rows(heights)[b]
    for r in range(h):
        scr[r + 1, LEFT : LEFT + w, :] = interior(r)
    lines = slice(b * 32, (b + 1) * 32)
    core, band = idx[0], idx[1] % 2
    for first, second, at in ((out_row, in_row, 0), (in_row, out_row, h + 1)):
        packed = pick(core, first[n, lines, :], second[n, lines, :])
        scr[at, LEFT : LEFT + w, :] = row_unpack(packed, c)
    for first, second, at in ((out_col, in_col, LEFT - 1), (in_col, out_col, LEFT + w)):
        vals = pick(band, first[n], second[n])
        for r in range(h):
            scr[r + 1, at : at + 1, :] = vals[start + r : start + r + 1, :c]
        scr[0, at : at + 1, :] = vals[16 + b : 17 + b, :c]
        scr[h + 1, at : at + 1, :] = vals[24 + b : 25 + b, :c]


def shifted(scr, h, w, q):
    return [scr[r, LEFT - 1 + q : LEFT - 1 + q + w, :].astype(BF) for r in range(h + 2)]


def side_by_side(scr, h, w, order):
    gap = jnp.zeros((w, 64 - scr.shape[2]), F32)
    rows = []
    for r in range(h + 2):
        parts = []
        for q in order:
            parts += [scr[r, LEFT - 1 + q : LEFT - 1 + q + w, :], gap]
        rows.append(jnp.concatenate(parts, axis=1).astype(BF))
    return rows


def apart(blocks, axis):
    parts = []
    for block in blocks:
        shape = list(block.shape)
        shape[axis] = 64 - shape[axis]
        parts += [block.astype(F32), jnp.zeros(shape, F32)]
    return jnp.concatenate(parts, axis=axis).astype(BF)


def forward_taps(scr, kernel, h, w):
    if scr.shape[2] <= 64:
        rows = side_by_side(scr, h, w, range(3))
        return sum(
            dot(stack(rows[p : p + h]), apart([kernel[p, q] for q in range(3)], 1), 1, 1)
            for p in range(3)
        )
    total = 0
    for q in range(3):
        rows = shifted(scr, h, w, q)
        total = total + sum(dot(stack(rows[p : p + h]), kernel[p, q], 1, 1) for p in range(3))
    return total


def adjoint_taps(scr, kernel, h, w):
    if scr.shape[2] <= 64:
        rows = side_by_side(scr, h, w, (2, 1, 0))
        return sum(
            dot(stack(rows[2 - p : 2 - p + h]), apart([kernel[p, q] for q in range(3)], 0))
            for p in range(3)
        )
    total = 0
    for q in range(3):
        rows = shifted(scr, h, w, 2 - q)
        total = total + sum(dot(stack(rows[2 - p : 2 - p + h]), kernel[p, q]) for p in range(3))
    return total


def weight_grads_kernel(dims, *refs):
    heights, widths, channels = dims
    idx, x_refs, sc_refs = refs[0], packed(dims, refs[1:4]), packed(dims, refs[4:7])
    edges = refs[7:11]
    keep, send, out, *scrs = refs[11:]
    c0, c1, c2 = channels[0], channels[1], channels[2]
    for b in (2, 1, 0):
        h, w, c = heights[b], widths[b], channels[b]
        fill(scrs[b], 0, b, dims, lambda r: jnp.maximum(x_refs[b][r].astype(F32), 0.0), idx, *edges)
        s_all = stack([sc_refs[b][r] for r in range(h)])
        if c <= 64:
            rows = side_by_side(scrs[b], h, w, range(3))
            wide = [dot(s_all, stack(rows[p : p + h]), 0, 0) for p in range(3)]
        for q in range(3):
            if c > 64:
                rows = shifted(scrs[b], h, w, q)
            for p in range(3):
                if c > 64:
                    g = dot(s_all, stack(rows[p : p + h]), 0, 0)
                else:
                    g = wide[p][:, 64 * q : 64 * q + c]
                tap = p * 3 + q
                if b == 2:
                    out[tap * c2 : (tap + 1) * c2, :] = g[:, :128].astype(BF)
                    half = c2 // 2
                    at = 9 * c2 + tap * half
                    both = jnp.concatenate([g[:half, 128:], g[half:, 128:]], axis=1)
                    out[at : at + half, :] = both.astype(BF)
                elif b == 1:
                    at = 9 * c2 * 3 // 2 + tap * c1
                    out[at : at + c1, :c1] = g.astype(BF)
                else:
                    at = 9 * c2 * 3 // 2 + 9 * c1 + (tap // 2) * c0
                    lane = 64 * (tap % 2)
                    out[at : at + c0, lane : lane + c0] = g.astype(BF)
    half = keep.shape[0]
    keep[...] = out[pl.ds(pl.multiple_of(idx[0] * half, 16), half), :]
    send[...] = out[pl.ds(pl.multiple_of((1 - idx[0]) * half, 16), half), :]


def pair_sum_kernel(n_branch, idx, keep, got, coarse, *outs):
    size = outs[0].shape[0]
    for k in range(n_branch):
        at = pl.ds(pl.multiple_of((idx[1] + k) % n_branch * size, 16), size)
        outs[k][...] = (keep[at, :].astype(F32) + got[at, :].astype(F32)).astype(BF)
    outs[-1][...] = coarse[...]


def stack_kernel(count, *refs):
    for k in range(count):
        refs[-1][k] = refs[k][...]


def corner_kernel(idx, sides, in_row, out_row, inner, outer):
    core, band = idx[0], idx[1] % 2
    cols = []
    for k, at in ((0, 128), (1, 136)):
        in_part, out_part = in_row[:, at : at + 8, :], out_row[:, at : at + 8, :]
        above, below = pick(core, out_part, in_part), pick(core, in_part, out_part)
        cols.append(jnp.concatenate([sides[k].astype(F32), above, below], axis=1))
    inner[...] = pick(band, cols[1], cols[0]).astype(BF)
    outer[...] = pick(band, cols[0], cols[1]).astype(BF)


def sum_kernel(count, *refs):
    total = refs[0][...].astype(F32)
    for k in range(1, count):
        total = total + refs[k][...].astype(F32)
    refs[-1][...] = total.astype(BF)


def ordered_sum_kernel(n, idx, *refs):
    held = refs[-1]
    for k in range(n):
        held[(idx[2] + k) % n] = refs[k][...]
    total = held[0].astype(F32)
    for k in range(1, n):
        total = total + held[k].astype(F32)
    refs[n][...] = total.astype(BF)


def forward_kernel(dims, idx, *refs):
    heights, widths, channels = dims
    x_refs = packed(dims, refs[0:4])
    g_refs, f_refs, k_refs = refs[4:8], refs[8:12], refs[12:16]
    edges = refs[16:20]
    refs = refs[20:]
    merged_refs, scrs, wide = refs[0:4], refs[4:8], refs[8:12]
    units = []
    for b in range(4):
        h, w, c = heights[b], widths[b], channels[b]
        fill(scrs[b], 0, b, dims, lambda r: jnp.maximum(x_refs[b][r].astype(F32), 0.0), idx, *edges)
        resp = forward_taps(scrs[b], k_refs[b], h, w)
        gain = gain_row(g_refs[b])
        units.append(
            [
                (x_refs[b][r].astype(F32) + gain * resp[r * w : (r + 1) * w]).astype(BF)
                for r in range(h)
            ]
        )
    mixers = [f_refs[j][...] for j in range(4)]

    def mix(v, j, i):
        off = source_offset(channels, j, i)
        if j == 3:
            return dot(v, mixers[3][off : off + channels[i]])
        return dot(v, mixers[j][:, off : off + channels[i]], 1, 1)

    sums = [[u.astype(F32) for u in units[j]] for j in range(4)]
    for i in range(4):
        for j in range(i + 1, 4):
            f = 2 ** (j - i)
            pool = group_matrix(widths[j], widths[i], f)
            for r in range(heights[j]):
                s = dot(pool, units[i][r * f])
                for k in range(1, f):
                    s = s + dot(pool, units[i][r * f + k])
                s = (s * (1.0 / (f * f))).astype(BF)
                sums[j][r] = sums[j][r] + mix(s, j, i)
        for j in range(i):
            f = 2 ** (i - j)
            spread = group_matrix(widths[i], widths[j], f, True)
            for r in range(heights[i]):
                v = mix(dot(spread, units[i][r]).astype(BF), j, i)
                for k in range(f):
                    sums[j][r * f + k] = sums[j][r * f + k] + v
    for j in range(4):
        emit(j, heights, merged_refs[j], sums[j], wide[j])


def emit(b, heights, out, rows, stage):
    if b >= 2:
        for r in range(heights[b]):
            out[r] = rows[r].astype(BF)
        flush(out)
        return
    for r in range(heights[b]):
        stage[r] = rows[r].T
    out[...] = jnp.swapaxes(stage[...], 0, 1).astype(BF)
    flush(out)


def adjoint_kernel(dims, idx, *refs):
    heights, widths, channels = dims
    x_refs, sc_refs, up_refs = (packed(dims, refs[k : k + 4]) for k in (0, 4, 8))
    k_refs = refs[12:16]
    edges = refs[16:20]
    refs = refs[20:]
    back_refs, scrs, wide = refs[0:4], refs[4:8], refs[8:12]
    for b in range(4):
        h, w, c = heights[b], widths[b], channels[b]
        fill(scrs[b], 1, b, dims, lambda r: sc_refs[b][r].astype(F32), idx, *edges)
        adj = adjoint_taps(scrs[b], k_refs[b], h, w)
        back = [
            up_refs[b][r].astype(F32)
            + jnp.where(x_refs[b][r].astype(F32) > 0, adj[r * w : (r + 1) * w], 0.0)
            for r in range(h)
        ]
        emit(b, heights, back_refs[b], back, wide[b])


def coarse_kernel(dims, n_branch, n_chip, scale, idx, *refs):
    out, act, win, grad, acc, taps, sems = refs[-7:]
    w3, c3 = dims[1][3], dims[2][3]
    rows, cols = 2 * n_chip, n_branch * w3
    act[0] = jnp.zeros(act.shape[1:], F32)
    act[rows + 1] = jnp.zeros(act.shape[1:], F32)
    for r in range(rows):
        act[r + 1, 0:LEFT, :] = jnp.zeros((LEFT, c3), F32)
        act[r + 1, LEFT + cols :, :] = jnp.zeros((8, c3), F32)
    for m in range(2):
        for l in range(n_branch):
            for k in range(n_chip):
                src = refs[m * n_branch + l]
                r = (idx[2] + k) % n_chip * 2 + (idx[0] + m) % 2
                off = pl.multiple_of((idx[1] + l) % n_branch * w3, w3)
                act[r + 1, pl.ds(LEFT + off, w3), :] = src[k, 0].astype(F32)
                win[r, pl.ds(off, w3), :] = src[k, 1]
    for r in range(rows):
        grad[:, r * cols : (r + 1) * cols] = win[r].astype(F32).T.astype(BF)
    span = rows * cols
    step = min(span, 1024)
    copies = []
    for q in range(3):
        for r in range(rows + 2):
            win[r] = act[r, LEFT - 1 + q : LEFT - 1 + q + cols, :].astype(BF)
        for p in range(3):
            if step == span:
                total = dot(grad[...], win[p : p + rows].reshape(span, c3))
            else:
                acc[...] = jnp.zeros(acc.shape, F32)
                lines = step // cols

                @pl.loop(0, rows // lines)
                def _(t, p=p):
                    some = win[pl.ds(t * lines + p, lines)].reshape(step, c3)
                    acc[...] += dot(grad[:, pl.ds(pl.multiple_of(t * step, step), step)], some)

                total = acc[...]
            taps[p, q] = (total * scale).astype(BF)
            copies.append(pltpu.make_async_copy(taps.at[p, q], out.at[p, q], sems.at[p, q]))
            copies[-1].start()
    for copy in copies:
        copy.wait()


def finish_kernel(dims, n_branch, scales, idx, *refs):
    channels = dims[2]
    own, other, *outs, flat = refs
    c0, c1, c2 = channels[0], channels[1], channels[2]
    size = own.shape[1]
    for k in range(n_branch):
        for part, core in ((own, idx[0]), (other, 1 - idx[0])):
            at = pl.multiple_of((core * n_branch + (idx[1] + k) % n_branch) * size, 16)
            flat[pl.ds(at, size), :] = part[k].astype(F32)
    base1 = 9 * c2 * 3 // 2
    base0 = base1 + 9 * c1
    half = c2 // 2
    for tap in range(9):
        p, q = tap // 3, tap % 3
        outs[2][p, q, :, 0:128] = (flat[tap * c2 : (tap + 1) * c2, :] * scales[2]).astype(BF)
        at = 9 * c2 + tap * half
        both = flat[at : at + half, :]
        tail = jnp.concatenate([both[:, :64], both[:, 64:]], axis=0)
        outs[2][p, q, :, 128:c2] = (tail * scales[2]).astype(BF)
        at = base1 + tap * c1
        outs[1][p, q] = (flat[at : at + c1, :c1] * scales[1]).astype(BF)
        at = base0 + (tap // 2) * c0
        lane = 64 * (tap % 2)
        outs[0][p, q] = (flat[at : at + c0, lane : lane + c0] * scales[0]).astype(BF)


def local(*args):
    maps, kernels, gains, mixers, cotans = (args[4 * k : 4 * k + 4] for k in range(5))
    n_rows, n_branch = lax.axis_size("rows"), lax.axis_size("branch")
    n_chip = n_rows // 2
    channels = [a.shape[0] for a in maps]
    heights = [a.shape[1] for a in maps]
    widths = [a.shape[2] for a in maps]
    dims = (heights, widths, channels)
    last = lambda a: jnp.transpose(a, (1, 2, 0))
    unlast = lambda a: jnp.transpose(a, (2, 0, 1))
    xs = [maps[0], maps[1], last(maps[2]), last(maps[3])]
    ds = [cotans[0], cotans[1], last(cotans[2]), last(cotans[3])]
    gs = [g.reshape(-1, 128) if g.shape[0] % 128 == 0 else g.reshape(1, -1) for g in gains]
    fs = [mixers[0], mixers[1], mixers[2], mixers[3].T]
    shapes = [(heights[b], widths[b], channels[b]) for b in range(4)]
    kept = [sds((h, w // 2, 128) if c <= 64 else (h, w, c), BF) for h, w, c in shapes]
    scales = [1.0 / math.sqrt(heights[b] * n_rows * widths[b] * n_branch) for b in range(4)]
    swap = lambda n: [(i, i ^ 1) for i in range(n)]
    hop = lambda n: [(i, i + 1 if i % 2 else i - 1) for i in range(1, n - 1)]
    core_swap = lambda a: lax.ppermute(a, "rows", swap(n_rows))
    from_branch = lambda k: [((i + k) % n_branch, i) for i in range(n_branch)]
    to_branch = lambda k: [(i, (i + k) % n_branch) for i in range(n_branch)]
    from_chip = lambda k: [((i + 2 * k) % n_rows, i) for i in range(n_rows)]

    outs = call(
        functools.partial(upstream_kernel, dims),
        kept * 3 + [sds((2, 144, PACK), BF)] * 2 + [sds((2, 2, 16, PACK), BF)]
        + [sds((2, heights[3] * widths[3], channels[3]), BF)],
        ds + fs + gs + xs,
        [pltpu.VMEM((2, 2, 144, PACK), BF)],
        placed=True, far=range(16), far_out=range(16), limit=WHOLE, flops=6 * 10**9,
    )
    xt, ups, scs = outs[:4], outs[4:8], outs[8:12]
    inner, outer, sides, coarse = outs[12:]
    out_row = lax.ppermute(outer, "rows", hop(n_rows))
    in_row = core_swap(inner)
    inner, outer = call(
        corner_kernel, [sds((2, 32, PACK), BF)] * 2, [sides, in_row, out_row],
        placed=True, flops=6 * 10**9,
    )
    out_col = lax.ppermute(outer, "branch", hop(n_branch))
    in_col = lax.ppermute(inner, "branch", swap(n_branch))
    edges = [in_row, out_row, in_col, out_col]

    pad = lambda b: pltpu.VMEM((heights[b] + 2, widths[b] + 16, channels[b]), F32)
    wide = [pltpu.VMEM((heights[b], channels[b], widths[b]), F32) for b in range(4)]
    pieces = 2 * n_branch
    packed_rows = 9 * (channels[2] * 3 // 2 + channels[1]) + 5 * channels[0]
    size = -(-packed_rows // (16 * pieces)) * 16
    part = sds((size, 128), BF)
    keep, send = call(
        functools.partial(weight_grads_kernel, dims),
        [sds((n_branch * size, 128), BF)] * 2,
        list(xt[:3]) + list(scs[:3]) + edges,
        [pltpu.VMEM((pieces * size, 128), BF), pad(0), pad(1), pad(2)],
        placed=True, flops=6 * 10**9,
    )
    *parts, coarse = call(
        functools.partial(pair_sum_kernel, n_branch),
        [part] * n_branch + [sds(coarse.shape, BF)],
        [keep, core_swap(send), coarse],
        placed=True,
    )
    got = [lax.ppermute(parts[k], "branch", to_branch(k)) for k in range(1, n_branch)]
    held = [coarse] + [lax.ppermute(coarse, "rows", from_chip(k)) for k in range(1, n_chip)]
    *back, back_token = call(
        functools.partial(adjoint_kernel, dims),
        [sds(maps[0].shape, BF), sds(maps[1].shape, BF), sds(shapes[2], BF), sds(shapes[3], BF)],
        list(xt) + list(scs) + list(ups) + list(kernels) + edges,
        [pad(b) for b in range(4)] + wide,
        placed=True, far_out=range(4), token=True, deps=(parts[0],), flops=ADJOINT,
    )
    (part_sum,) = call(
        functools.partial(sum_kernel, n_branch), [part], [parts[0]] + got, deps=(back_token, *held[1:])
    )
    got = [lax.ppermute(part_sum, "rows", from_chip(k)) for k in range(1, n_chip)]
    (held,) = call(
        functools.partial(stack_kernel, n_chip), [sds((n_chip,) + coarse.shape, BF)], held,
        deps=(part_sum,),
    )
    held = [held] + [lax.ppermute(held, "branch", from_branch(k)) for k in range(1, n_branch)]
    *merged, merged_token = call(
        functools.partial(forward_kernel, dims),
        [sds(maps[0].shape, BF), sds(maps[1].shape, BF), sds(shapes[2], BF), sds(shapes[3], BF)],
        list(xt) + gs + fs + list(kernels) + edges,
        [pad(b) for b in range(4)] + wide,
        placed=True, far_out=range(4), token=True, deps=(part_sum,), flops=FORWARD,
    )
    (total,) = call(
        functools.partial(ordered_sum_kernel, n_chip), [part], [part_sum] + got,
        [pltpu.VMEM((n_chip, size, 128), BF)], placed=True, deps=(merged_token, *held[1:]),
    )
    mine = [total] + [lax.ppermute(total, "branch", from_branch(k)) for k in range(1, n_branch)]
    held = held + [core_swap(a) for a in held]
    cols = n_branch * widths[3]
    kgrad3, coarse_token = call(
        functools.partial(coarse_kernel, dims, n_branch, n_chip, scales[3]),
        [sds(kernels[3].shape, BF)],
        held,
        [
            pltpu.VMEM((n_rows + 2, cols + 16, channels[3]), F32),
            pltpu.VMEM((n_rows + 2, cols, channels[3]), BF),
            pltpu.VMEM((channels[3], n_rows * cols), BF),
            pltpu.VMEM((channels[3], channels[3]), F32),
            pltpu.VMEM(kernels[3].shape, BF),
            pltpu.SemaphoreType.DMA((3, 3)),
        ],
        placed=True, raw_out=(0,), token=True, deps=(total,), flops=GATHERED, limit=COARSE,
    )
    (mine,) = call(
        functools.partial(stack_kernel, n_branch), [sds((n_branch, size, 128), BF)], mine,
        deps=(coarse_token, back_token,),
    )
    kgrads = call(
        functools.partial(finish_kernel, dims, n_branch, scales),
        [sds(k.shape, BF) for k in kernels[:3]],
        [mine, core_swap(mine)],
        [pltpu.VMEM((pieces * size, 128), F32)], placed=True, far_out=range(3),
    )
    return (
        merged[0], merged[1], unlast(merged[2]), unlast(merged[3]),
        back[0], back[1], unlast(back[2]), unlast(back[3]),
        *kgrads, kgrad3,
    )


def solution(mesh):
    maps = P(None, "rows", "branch")
    in_specs = (maps,) * 4 + (P(),) * 12 + (maps,) * 4
    out_specs = (maps,) * 8 + (P(),) * 4
    return jax.shard_map(
        lambda *args: local(*args),
        mesh=mesh, in_specs=in_specs, out_specs=out_specs, check_vma=False,
    )
```
